32 devices in a mesh: sky: 8 (over z, y), visit: 4 (over x, core).
Axes of the slice: x: 2, y: 2, z: 4, core: 2. Of those that a mesh axis runs over, the one named last changes fastest.
Arguments:
- science: float32 [32, 512, 256], P('visit', 'sky'), may hold values from -6 to 6
- inv_variance: float32 [32, 512, 256], P('visit', 'sky'), may hold values from 0.3 to 3
- psf_kernel: float32 [11, 11], replicated, may hold values from 0.01 to 0.12
- offsets: int32 [32, 16], replicated, may hold values from -2 to 2, as said below
Outputs:
- likelihood: float32 [16, 512, 256], P(None, ('sky', 'visit'))
The draws below stay inside these ranges and needn't reach their ends.
Inputs may be any that keep to these rules, and one draw needn't show every extreme that they name: offsets[0, k] is 0 for every velocity; offsets[31, 0] is 2 and offsets[31, 1] is -2.
All inputs are finite; a program needn't handle non-finite values.
Results may differ from the reference program's by a relative error of at most 0.0001.
Values sent between devices are 32-bit elements; how exact they have to be, the bound alone decides.
A program may use at most 64 MiB of HBM per device.

```python
import math
import jax
import jax.numpy as jnp
from jax import lax

V = 32
K = 16
PR = 5
BR = 8
MAXOFF = 2
W = 256
H = 512


def draw_offsets(key, part):
    drawn = jax.random.randint(key, (V, K), -MAXOFF, MAXOFF + 1)
    drawn = drawn.at[0, :].set(0)
    drawn = drawn.at[V - 1, 0].set(MAXOFF)
    drawn = drawn.at[V - 1, 1].set(-MAXOFF)
    return drawn.astype(jnp.int32)


def steps_of(own_key, shape, shards, smallest, high):
    loudness, own = 1.0, jax.random.fold_in(own_key, 6)
    for dim, shards_of in shards:
        heights = jnp.exp(jax.random.uniform(jax.random.fold_in(own, dim), (shards_of,), jnp.float32, smallest / len(shards), high / len(shards)))
        loudness = loudness * jnp.repeat(heights, shape[dim] // shards_of).reshape([-1 if axis == dim else 1 for axis in range(len(shape))])
    return loudness


def bell_draw(stream_key, dims, width, limit, split=(), kind=jnp.bfloat16):
    values = width * jax.random.normal(stream_key, dims, jnp.float32)
    if split:
        values = values * steps_of(stream_key, dims, split, -0.22, 0.18)
    return jnp.clip(values, -limit, limit).astype(kind)


def setup_inputs(seed: int = 0) -> dict:
    streams_of = jax.random.split(jax.random.key(seed), 5)
    return {
        "science": bell_draw(streams_of[0], (V, H, W), 1.0, 6.0, ((0, 4), (1, 8)), jnp.float32),
        "inv_variance": jnp.clip(jnp.exp(math.log(3.0) - 2.3025851 * jax.random.uniform(streams_of[1], (V, H, W), jnp.float32) ** steps_of(streams_of[1], (V, H, W), ((0, 4), (1, 8)), -0.2, 0.2)), 0.3, 3.0),
        "psf_kernel": jnp.clip(jnp.exp(jax.random.uniform(streams_of[2], (2 * PR + 1, 2 * PR + 1), jnp.float32, math.log(0.01), math.log(0.12))), 0.01, 0.12),
        "offsets": draw_offsets(jax.random.fold_in(streams_of[4], 71), 0),
    }


def reference(science, inv_variance, psf_kernel, offsets):
    radius = (psf_kernel.shape[0] - 1) // 2
    kernel_size = 2 * radius + 1
    weights = jnp.stack([psf_kernel, psf_kernel * psf_kernel])

    def correlate_visit(visit_pair):
        sci_rows, inv_rows = visit_pair
        paired = jnp.stack([sci_rows * inv_rows, inv_rows])
        padded = jnp.pad(paired, ((0, 0), (radius, radius), (radius, radius)))
        running = jnp.zeros(paired.shape, jnp.float32)
        for row_tap in range(kernel_size):
            for col_tap in range(kernel_size):
                running = running + weights[:, row_tap, col_tap][:, None, None] * padded[:, row_tap:row_tap + H, col_tap:col_tap + W]
        return running
    images = lax.map(correlate_visit, (science, inv_variance))
    reach_rows = MAXOFF * BR
    padded = jnp.pad(images, ((0, 0), (0, 0), (reach_rows, reach_rows), (0, 0)))
    stacked = jnp.zeros((2, K, H, W), jnp.float32)
    for offset_value in range(-MAXOFF, MAXOFF + 1):
        onehot = (offsets == offset_value).astype(jnp.float32)
        start_row = reach_rows + offset_value * BR
        window = padded[:, :, start_row:start_row + H, :]
        stacked = stacked + jnp.einsum('tk,tcrw->ckrw', onehot, window, precision=lax.Precision.HIGHEST)
    return stacked[0] / jnp.sqrt(stacked[1])
```

```python
import jax
import jax.numpy as jnp
from jax import lax
from jax.experimental import pallas as pl
from jax.experimental.pallas import tpu as pltpu
from jax.sharding import PartitionSpec as P

BR = 8
MAXOFF = 2
MESH = pl.DeviceIdType.MESH
F32 = jnp.float32
BF16 = jnp.bfloat16


def build_bands(psf_ref, taps, size, bands):
    radius = size // 2
    half = 128
    for image in range(2):
        for part in range(2):
            bands[image, part, :, 0:half, half:] = jnp.zeros((size, half, half), BF16)
            bands[image, part, :, half:, 0:half] = jnp.zeros((size, half, half), BF16)

    def fill(a, carry):
        def place(rows, cols, shift, spots):
            diff = (
                lax.broadcasted_iota(jnp.int32, (rows, cols), 0)
                - lax.broadcasted_iota(jnp.int32, (rows, cols), 1)
                + shift
            )
            value = jnp.zeros((rows, cols), F32)
            for b in range(size):
                value = jnp.where(diff == b - radius, psf_ref[a, b], value)
            for image in range(2):
                full = value if image == 0 else value * value
                high = full.astype(BF16)
                low = (full - high.astype(F32)).astype(BF16)
                for row, col in spots:
                    bands[image, 0, a, row : row + rows, col : col + cols] = high
                    bands[image, 1, a, row : row + rows, col : col + cols] = low

        place(half, half, 0, ((0, 0), (half, half)))
        place(16, half, -16, ((half - 16, half),))
        place(16, half, half, ((half, 0),))
        return carry

    lax.fori_loop(0, size, fill, 0)


def kernel(
    sky_count,
    psf_ref,
    off_ref,
    sci_ref,
    inv_ref,
    out_ref,
    raw,
    high,
    low,
    bands,
    own,
    edge,
    part_send,
    part_own,
    part_recv,
    x_recv,
    raw_send_sem,
    raw_recv_sem,
    img_send_sem,
    img_recv_sem,
    core_send_sem,
    core_recv_sem,
    x_sems,
):
    visits, rows, cols = sci_ref.shape
    size = psf_ref.shape[0]
    radius = size // 2
    group = rows // 4
    gb, rb = group // BR, rows // BR
    sky = lax.axis_index("sky")
    me = lax.axis_index("visit")
    far, near = lax.div(me, 2), lax.rem(me, 2)
    mate = (sky, 2 * far + 1 - near)
    across = (sky, 2 * (1 - far) + near)
    above, below = (sky - 1, me), (sky + 1, me)
    has_above, has_below = sky > 0, sky < sky_count - 1

    barrier = pltpu.get_barrier_semaphore()
    pl.semaphore_signal(barrier, inc=1, device_id=mate, device_id_type=MESH)
    pl.semaphore_signal(barrier, inc=1, device_id=across, device_id_type=MESH)

    @pl.when(has_above)
    def _():
        pl.semaphore_signal(barrier, inc=1, device_id=above, device_id_type=MESH)

    @pl.when(has_below)
    def _():
        pl.semaphore_signal(barrier, inc=1, device_id=below, device_id_type=MESH)

    def turn(i, carry):
        at = pl.multiple_of(i * 8, 8)
        variance = inv_ref[:, pl.ds(at, 8), :]
        weighted = sci_ref[:, pl.ds(at, 8), :] * variance
        raw[0, pl.ds(radius + at, 8)] = jnp.swapaxes(weighted, 0, 1)
        raw[1, pl.ds(radius + at, 8)] = jnp.swapaxes(variance, 0, 1)
        return carry

    lax.fori_loop(0, rows // 8, turn, 0)

    pl.semaphore_wait(barrier, 2 + has_above.astype(jnp.int32) + has_below.astype(jnp.int32))

    def remote(src, dst, send_sem, recv_sem, device):
        return pltpu.make_async_remote_copy(
            src_ref=src,
            dst_ref=dst,
            send_sem=send_sem,
            recv_sem=recv_sem,
            device_id=device,
            device_id_type=MESH,
        )

    raw_up = remote(
        raw.at[:, radius : 2 * radius],
        raw.at[:, rows + radius : rows + 2 * radius],
        raw_send_sem.at[0],
        raw_recv_sem.at[0],
        above,
    )
    raw_down = remote(
        raw.at[:, rows : rows + radius],
        raw.at[:, 0:radius],
        raw_send_sem.at[1],
        raw_recv_sem.at[1],
        below,
    )

    @pl.when(has_above)
    def _():
        raw_up.start()

    @pl.when(has_below)
    def _():
        raw_down.start()

    @pl.when(jnp.logical_not(has_above))
    def _():
        raw[:, 0:radius] = jnp.zeros((2, radius, visits, cols), F32)
        edge[0, :, :, 0:MAXOFF] = jnp.zeros((2, visits, MAXOFF, BR, cols), F32)

    @pl.when(jnp.logical_not(has_below))
    def _():
        raw[:, rows + radius :] = jnp.zeros((2, radius, visits, cols), F32)
        edge[1, :, :, gb + MAXOFF :] = jnp.zeros((2, visits, MAXOFF, BR, cols), F32)

    build_bands(psf_ref, size, size, bands)

    @pl.when(has_above)
    def _():
        raw_down.wait_recv()

    @pl.when(has_below)
    def _():
        raw_up.wait_recv()

    def split(i, carry):
        for image in range(2):
            for odd in range(2):
                pair = raw[image, pl.ds(2 * i + odd, 2)].reshape(2 * visits, cols)
                first = pair.astype(BF16)
                high[image, odd, i] = first
                low[image, odd, i] = (pair - first.astype(F32)).astype(BF16)
        return carry

    pairs = (rows + 2 * radius) // 2
    lax.fori_loop(0, pairs - 1, split, 0)
    for image in range(2):
        pair = raw[image, rows + 2 * radius - 2 :].reshape(2 * visits, cols)
        first = pair.astype(BF16)
        high[image, 0, pairs - 1] = first
        low[image, 0, pairs - 1] = (pair - first.astype(F32)).astype(BF16)

    def correlate(image, starts, count):
        total = jnp.zeros((len(starts) * count * visits, cols), F32)
        for a in range(size):
            def rows_of(terms):
                pieces = [
                    terms[image, a % 2, (start + a) // 2 : (start + a) // 2 + count // 2].reshape(
                        count * visits, cols
                    )
                    for start in starts
                ]
                return pieces[0] if len(pieces) == 1 else jnp.concatenate(pieces, axis=0)

            x_high, x_low = rows_of(high), rows_of(low)
            w_high, w_low = bands[image, 0, a], bands[image, 1, a]
            total = total + jnp.dot(x_high, w_high, preferred_element_type=F32)
            total = total + jnp.dot(x_low, w_high, preferred_element_type=F32)
            total = total + jnp.dot(x_high, w_low, preferred_element_type=F32)
        turned = jnp.swapaxes(total.reshape(len(starts) * count, visits, cols), 0, 1)
        return turned.reshape(visits, len(starts) * count // BR, BR, cols)

    img_up = [
        remote(
            own.at[image, :, 0:MAXOFF],
            edge.at[1, image, :, gb + MAXOFF : gb + 2 * MAXOFF],
            img_send_sem.at[0, image],
            img_recv_sem.at[0, image],
            above,
        )
        for image in range(2)
    ]
    img_down = [
        remote(
            own.at[image, :, rb - MAXOFF : rb],
            edge.at[0, image, :, 0:MAXOFF],
            img_send_sem.at[1, image],
            img_recv_sem.at[1, image],
            below,
        )
        for image in range(2)
    ]

    for image in range(2):
        value = correlate(image, (0, rows - group), group)
        own[image, :, 0:gb] = value[:, 0:gb]
        own[image, :, rb - gb : rb] = value[:, gb:]
        edge[0, image, :, MAXOFF : MAXOFF + gb] = value[:, 0:gb]
        edge[1, image, :, MAXOFF : MAXOFF + gb] = value[:, gb:]

        @pl.when(has_above)
        def _():
            img_up[image].start()

        @pl.when(has_below)
        def _():
            img_down[image].start()

    for image in range(2):
        value = correlate(image, (group,), rows - 2 * group)
        own[image, :, gb : rb - gb] = value
        edge[0, image, :, MAXOFF + gb :] = value[:, 0:MAXOFF]
        edge[1, image, :, 0:MAXOFF] = value[:, rb - 2 * gb - MAXOFF :]

    def stack(load, base, target):
        def velocity(k, carry):
            totals = [[None] * gb, [None] * gb]
            for t in range(visits):
                first = base + off_ref[me * visits + t, k]
                for image in range(2):
                    for block in range(gb):
                        term = load(image, t, first + block)
                        held = totals[image][block]
                        totals[image][block] = term if held is None else held + term
            for image in range(2):
                for block in range(gb):
                    target[image, k, block] = totals[image][block]
            return carry

        lax.fori_loop(0, out_ref.shape[0], velocity, 0)

    def own_rows(image, t, block):
        return own[image, t, block]

    core = [
        remote(
            part_send.at[stage],
            part_recv.at[stage],
            core_send_sem.at[stage],
            core_recv_sem.at[stage],
            mate,
        )
        for stage in range(2)
    ]
    hop = [remote(part_own.at[stage], x_recv, x_sems.at[0], x_sems.at[1], across) for stage in range(2)]

    def gather(stage):
        def add(k, carry):
            for image in range(2):
                part_own[stage, image, k] += part_recv[stage, image, k]
            return carry

        lax.fori_loop(0, out_ref.shape[0], add, 0)

    stack(own_rows, (1 + near) * gb, part_send.at[0])
    core[0].start()
    stack(own_rows, (2 - near) * gb, part_own.at[0])
    core[0].wait_recv()
    gather(0)

    @pl.when(far == near)
    def _():
        hop[0].start()

    for image in range(2):

        @pl.when(has_above)
        def _():
            img_down[image].wait_recv()

        @pl.when(has_below)
        def _():
            img_up[image].wait_recv()

    stack(lambda image, t, block: edge[1 - near, image, t, block], MAXOFF, part_send.at[1])
    core[1].start()
    stack(lambda image, t, block: edge[near, image, t, block], MAXOFF, part_own.at[1])
    core[1].wait_recv()
    gather(1)

    @pl.when(far != near)
    def _():
        hop[1].start()

    hop[0].wait_recv()

    def finish(stage):
        def velocity(k, carry):
            top = part_own[stage, 0, k] + x_recv[0, k]
            bottom = part_own[stage, 1, k] + x_recv[1, k]
            out_ref[k] = (top / jnp.sqrt(bottom)).reshape(group, cols)
            return carry

        lax.fori_loop(0, out_ref.shape[0], velocity, 0)

    @pl.when(far == near)
    def _():
        finish(1)

    @pl.when(far != near)
    def _():
        finish(0)

    @pl.when(has_above)
    def _():
        raw_up.wait_send()
        img_up[0].wait_send()
        img_up[1].wait_send()

    @pl.when(has_below)
    def _():
        raw_down.wait_send()
        img_down[0].wait_send()
        img_down[1].wait_send()

    core[0].wait_send()
    core[1].wait_send()
    hop[0].wait_send()


def solution(mesh):
    sky_count = mesh.shape["sky"]

    def shards(science, inv_variance, psf_kernel, offsets):
        visits, rows, cols = science.shape
        size = psf_kernel.shape[0]
        velocities = offsets.shape[1]
        radius, group = size // 2, rows // 4
        depth = rows + 2 * radius
        vmem = pl.BlockSpec(memory_space=pltpu.VMEM)
        smem = pl.BlockSpec(memory_space=pltpu.SMEM)
        parts = (2, 2, velocities, group // BR, BR, cols)
        dma = pltpu.SemaphoreType.DMA

        def body(*refs):
            kernel(sky_count, *refs)

        return pl.pallas_call(
            body,
            out_shape=jax.ShapeDtypeStruct((velocities, group, cols), F32),
            in_specs=[smem, smem, vmem, vmem],
            out_specs=vmem,
            scratch_shapes=[
                pltpu.VMEM((2, depth, visits, cols), F32),
                pltpu.VMEM((2, 2, depth // 2, 2 * visits, cols), BF16),
                pltpu.VMEM((2, 2, depth // 2, 2 * visits, cols), BF16),
                pltpu.VMEM((2, 2, size, cols, cols), BF16),
                pltpu.VMEM((2, visits, rows // BR, BR, cols), F32),
                pltpu.VMEM((2, 2, visits, group // BR + 2 * MAXOFF, BR, cols), F32),
                pltpu.VMEM(parts, F32),
                pltpu.VMEM(parts, F32),
                pltpu.VMEM(parts, F32),
                pltpu.VMEM(parts[1:], F32),
                dma((2,)),
                dma((2,)),
                dma((2, 2)),
                dma((2, 2)),
                dma((2,)),
                dma((2,)),
                dma((2,)),
            ],
            compiler_params=pltpu.CompilerParams(
                collective_id=0, has_side_effects=True, vmem_limit_bytes=48 * 1024 * 1024
            ),
        )(psf_kernel, offsets, science, inv_variance)

    return jax.shard_map(
        shards,
        mesh=mesh,
        in_specs=(P("visit", "sky", None), P("visit", "sky", None), P(), P()),
        out_specs=P(None, ("sky", "visit"), None),
        check_vma=False,
    )
```

```python
import jax
import jax.numpy as jnp
from jax import lax
from jax.experimental import pallas as pl
from jax.experimental.pallas import tpu as pltpu
from jax.sharding import PartitionSpec as P

BR = 8
MAXOFF = 2
MESH = pl.DeviceIdType.MESH
F32 = jnp.float32
BF16 = jnp.bfloat16


def build_bands(psf_ref, taps, size, bands):
    radius = size // 2
    half = 128
    for image in range(2):
        for part in range(2):
            bands[image, part, :, 0:half, half:] = jnp.zeros((size, half, half), BF16)
            bands[image, part, :, half:, 0:half] = jnp.zeros((size, half, half), BF16)

    def fill(a, carry):
        def place(rows, cols, shift, spots):
            diff = (
                lax.broadcasted_iota(jnp.int32, (rows, cols), 0)
                - lax.broadcasted_iota(jnp.int32, (rows, cols), 1)
                + shift
            )
            value = jnp.zeros((rows, cols), F32)
            for b in range(size):
                value = jnp.where(diff == b - radius, psf_ref[a, b], value)
            for image in range(2):
                full = value if image == 0 else value * value
                high = full.astype(BF16)
                low = (full - high.astype(F32)).astype(BF16)
                for row, col in spots:
                    bands[image, 0, a, row : row + rows, col : col + cols] = high
                    bands[image, 1, a, row : row + rows, col : col + cols] = low

        place(half, half, 0, ((0, 0), (half, half)))
        place(16, half, -16, ((half - 16, half),))
        place(16, half, half, ((half, 0),))
        return carry

    lax.fori_loop(0, size, fill, 0)


def kernel(
    sky_count,
    psf_ref,
    off_ref,
    sci_hbm,
    inv_hbm,
    out_ref,
    sci_ref,
    inv_ref,
    raw,
    high,
    low,
    bands,
    images,
    part_send,
    part_own,
    part_recv,
    x_recv,
    load_sems,
    raw_send_sem,
    raw_recv_sem,
    core_send_sem,
    core_recv_sem,
    x_send_sem,
    x_recv_sem,
):
    visits, rows, cols = sci_ref.shape
    size = psf_ref.shape[0]
    radius = size // 2
    halo = radius + MAXOFF * BR
    blocks = rows // BR
    velocities = off_ref.shape[0]
    sky = lax.axis_index("sky")
    me = lax.axis_index("visit")
    far, near = lax.div(me, 2), lax.rem(me, 2)
    mate = (sky, 2 * far + 1 - near)
    across = (sky, 2 * (1 - far) + near)
    above, below = (sky - 1, me), (sky + 1, me)
    has_above, has_below = sky > 0, sky < sky_count - 1

    load_sci = pltpu.make_async_copy(sci_hbm, sci_ref, load_sems.at[0])
    load_inv = pltpu.make_async_copy(inv_hbm, inv_ref, load_sems.at[1])
    load_sci.start()
    load_inv.start()

    barrier = pltpu.get_barrier_semaphore()
    pl.semaphore_signal(barrier, inc=1, device_id=mate, device_id_type=MESH)
    pl.semaphore_signal(barrier, inc=1, device_id=across, device_id_type=MESH)

    @pl.when(has_above)
    def _():
        pl.semaphore_signal(barrier, inc=1, device_id=above, device_id_type=MESH)

    @pl.when(has_below)
    def _():
        pl.semaphore_signal(barrier, inc=1, device_id=below, device_id_type=MESH)

    def turn(first, count):
        def block(i, carry):
            at = pl.multiple_of(i * BR, BR)
            variance = inv_ref[:, pl.ds(at, BR), :]
            weighted = sci_ref[:, pl.ds(at, BR), :] * variance
            raw[0, pl.ds(halo + at, BR)] = jnp.swapaxes(weighted, 0, 1)
            raw[1, pl.ds(halo + at, BR)] = jnp.swapaxes(variance, 0, 1)
            return carry

        lax.fori_loop(first, first + count, block, 0)

    def remote(src, dst, send_sem, recv_sem, device):
        return pltpu.make_async_remote_copy(
            src_ref=src,
            dst_ref=dst,
            send_sem=send_sem,
            recv_sem=recv_sem,
            device_id=device,
            device_id_type=MESH,
        )

    def raw_copy(way, chunk, source, target, count, device):
        return remote(
            raw.at[:, source : source + count],
            raw.at[:, target : target + count],
            raw_send_sem.at[way, chunk],
            raw_recv_sem.at[way, chunk],
            device,
        )

    inner = halo - BR
    up = [
        raw_copy(0, 0, halo, halo + rows, inner, above),
        raw_copy(0, 1, halo + inner, halo + rows + inner, BR, above),
    ]
    down = [
        raw_copy(1, 0, halo + rows - inner, BR, inner, below),
        raw_copy(1, 1, rows, 0, BR, below),
    ]
    edge_blocks = (halo + BR - 1) // BR

    load_sci.wait()
    load_inv.wait()
    turn(0, edge_blocks)
    turn(blocks - edge_blocks, edge_blocks)
    pl.semaphore_wait(barrier, 2 + has_above.astype(jnp.int32) + has_below.astype(jnp.int32))

    for chunk in range(2):

        @pl.when(has_above)
        def _():
            up[chunk].start()

        @pl.when(has_below)
        def _():
            down[chunk].start()

    @pl.when(jnp.logical_not(has_above))
    def _():
        raw[:, 0:halo] = jnp.zeros((2, halo, visits, cols), F32)

    @pl.when(jnp.logical_not(has_below))
    def _():
        raw[:, halo + rows :] = jnp.zeros((2, halo, visits, cols), F32)

    turn(edge_blocks, blocks - 2 * edge_blocks)
    build_bands(psf_ref, size, size, bands)

    def split(odd, first, last):
        def pair_of(i, carry):
            for image in range(2):
                pair = raw[image, pl.ds(2 * i + odd, 2)].reshape(2 * visits, cols)
                head = pair.astype(BF16)
                high[image, odd, i] = head
                low[image, odd, i] = (pair - head.astype(F32)).astype(BF16)
            return carry

        lax.fori_loop(first, last, pair_of, 0)

    def correlate(starts, count):
        def image_of(image, carry):
            total = jnp.zeros((len(starts) * count * visits, cols), F32)
            for a in range(size):

                def rows_of(terms):
                    pieces = [
                        terms[image, a % 2, (start + a) // 2 : (start + a) // 2 + count // 2].reshape(
                            count * visits, cols
                        )
                        for start in starts
                    ]
                    return pieces[0] if len(pieces) == 1 else jnp.concatenate(pieces, axis=0)

                x_high, x_low = rows_of(high), rows_of(low)
                w_high, w_low = bands[image, 0, a], bands[image, 1, a]
                total = total + jnp.dot(x_high, w_high, preferred_element_type=F32)
                total = total + jnp.dot(x_low, w_high, preferred_element_type=F32)
                total = total + jnp.dot(x_high, w_low, preferred_element_type=F32)
            value = jnp.swapaxes(total.reshape(len(starts) * count, visits, cols), 0, 1)
            value = value.reshape(visits, len(starts) * count // BR, BR, cols)
            many = count // BR
            for i, start in enumerate(starts):
                images[image, :, start // BR : start // BR + many] = value[:, i * many : (i + 1) * many]
            return carry

        lax.fori_loop(0, 2, image_of, 0)

    def stack(block, target):
        def velocity(k, carry):
            totals = [None, None]
            for t in range(visits):
                place = block + MAXOFF + off_ref[k, me * visits + t]
                for image in range(2):
                    term = images[image, t, place]
                    totals[image] = term if t == 0 else totals[image] + term
            target[0, k] = totals[0]
            target[1, k] = totals[1]
            return carry

        lax.fori_loop(0, velocities, velocity, 0)

    core = [
        remote(
            part_send.at[stage],
            part_recv.at[stage],
            core_send_sem.at[stage],
            core_recv_sem.at[stage],
            mate,
        )
        for stage in range(4)
    ]
    hop = [
        remote(
            part_own.at[stage],
            x_recv.at[stage % 2],
            x_send_sem.at[stage % 2],
            x_recv_sem.at[stage % 2],
            across,
        )
        for stage in range(4)
    ]
    middle, last = blocks // 2, blocks - 1
    mine = [
        middle - near,
        middle + 1 - 3 * near,
        1 + (last - 2) * near,
        last * near,
    ]
    other = [last - block for block in mine]
    early_goes = far == near

    def give(stage):
        stack(other[stage], part_send.at[stage])
        core[stage].start()

    def keep(stage):
        stack(mine[stage], part_own.at[stage])

    def gather(stage):
        core[stage].wait_recv()

        def add(k, carry):
            for image in range(2):
                part_own[stage, image, k] += part_recv[stage, image, k]
            return carry

        lax.fori_loop(0, velocities, add, 0)

        @pl.when(early_goes if stage < 2 else jnp.logical_not(early_goes))
        def _():
            hop[stage].start()

    def arrived(chunk):
        @pl.when(has_above)
        def _():
            down[chunk].wait_recv()

        @pl.when(has_below)
        def _():
            up[chunk].wait_recv()

    def outside(block):
        @pl.when(jnp.logical_not(has_above))
        def _():
            images[:, :, block] = jnp.zeros((2, visits, BR, cols), F32)

        @pl.when(jnp.logical_not(has_below))
        def _():
            images[:, :, blocks + 2 * MAXOFF - 1 - block] = jnp.zeros((2, visits, BR, cols), F32)

    depth = rows + 2 * halo
    total_blocks = blocks + 2 * MAXOFF
    lead = 3 * BR
    lo, hi = lead // 2, (depth - lead) // 2
    split(0, lo, hi)
    split(1, lo, hi)
    correlate((lead,), rows + 2 * MAXOFF * BR - 2 * lead)
    give(0)
    keep(0)
    gather(0)

    arrived(0)
    lo1, hi1 = BR // 2, (depth - BR) // 2
    split(0, lo1, lo)
    split(1, lo1, lo)
    split(0, hi, hi1)
    split(1, hi, hi1 - 1)
    correlate((BR, (total_blocks - 3) * BR), 2 * BR)
    outside(1)
    give(1)
    give(2)
    keep(1)
    gather(1)
    keep(2)
    gather(2)

    arrived(1)
    split(0, 0, lo1)
    split(1, 0, lo1)
    split(0, hi1, depth // 2)
    split(1, hi1 - 1, depth // 2 - 1)
    correlate((0, (total_blocks - 1) * BR), BR)
    outside(0)
    give(3)
    keep(3)
    gather(3)

    def finish(stage, place):
        hop[stage].wait_recv()

        def velocity(k, carry):
            top = part_own[stage, 0, k] + x_recv[stage % 2, 0, k]
            bottom = part_own[stage, 1, k] + x_recv[stage % 2, 1, k]
            out_ref[k, place] = top / jnp.sqrt(bottom)
            return carry

        lax.fori_loop(0, velocities, velocity, 0)

    @pl.when(early_goes)
    def _():
        finish(2, 1 - near)
        finish(3, near)

    @pl.when(jnp.logical_not(early_goes))
    def _():
        finish(0, near)
        finish(1, 1 - near)

    for chunk in range(2):

        @pl.when(has_above)
        def _():
            up[chunk].wait_send()

        @pl.when(has_below)
        def _():
            down[chunk].wait_send()

    for stage in range(4):
        core[stage].wait_send()
    hop[0].wait_send()
    hop[1].wait_send()


def solution(mesh):
    sky_count = mesh.shape["sky"]

    def shards(science, inv_variance, psf_kernel, offsets):
        visits, rows, cols = science.shape
        size = psf_kernel.shape[0]
        velocities = offsets.shape[1]
        group = rows // 4
        depth = rows + 2 * (size // 2 + MAXOFF * BR)
        hbm = pl.BlockSpec(memory_space=pltpu.HBM)
        vmem = pl.BlockSpec(memory_space=pltpu.VMEM)
        smem = pl.BlockSpec(memory_space=pltpu.SMEM)
        parts = (4, 2, velocities, BR, cols)
        dma = pltpu.SemaphoreType.DMA

        def body(*refs):
            kernel(sky_count, *refs)

        stacked = pl.pallas_call(
            body,
            out_shape=jax.ShapeDtypeStruct((velocities, group // BR, BR, cols), F32),
            in_specs=[smem, smem, hbm, hbm],
            out_specs=vmem,
            scratch_shapes=[
                pltpu.VMEM((visits, rows, cols), F32),
                pltpu.VMEM((visits, rows, cols), F32),
                pltpu.VMEM((2, depth, visits, cols), F32),
                pltpu.VMEM((2, 2, depth // 2, 2 * visits, cols), BF16),
                pltpu.VMEM((2, 2, depth // 2, 2 * visits, cols), BF16),
                pltpu.VMEM((2, 2, size, cols, cols), BF16),
                pltpu.VMEM((2, visits, rows // BR + 2 * MAXOFF, BR, cols), F32),
                pltpu.VMEM(parts, F32),
                pltpu.VMEM(parts, F32),
                pltpu.VMEM(parts, F32),
                pltpu.VMEM((2,) + parts[1:], F32),
                dma((2,)),
                dma((2, 2)),
                dma((2, 2)),
                dma((4,)),
                dma((4,)),
                dma((2,)),
                dma((2,)),
            ],
            compiler_params=pltpu.CompilerParams(
                collective_id=0, has_side_effects=True, vmem_limit_bytes=48 * 1024 * 1024
            ),
        )(psf_kernel, offsets.T, science, inv_variance)
        return stacked.reshape(velocities, group, cols)

    return jax.shard_map(
        shards,
        mesh=mesh,
        in_specs=(P("visit", "sky", None), P("visit", "sky", None), P(), P()),
        out_specs=P(None, ("sky", "visit"), None),
        check_vma=False,
    )
```

```python
import jax
import jax.numpy as jnp
from jax import lax
from jax.experimental import pallas as pl
from jax.experimental.pallas import tpu as pltpu
from jax.sharding import PartitionSpec as P

BR = 8
MAXOFF = 2
MESH = pl.DeviceIdType.MESH
F32 = jnp.float32
BF16 = jnp.bfloat16


def build_bands(psf_ref, taps, size, bands):
    radius = size // 2
    half = 128
    for image in range(2):
        for part in range(2):
            bands[image, part, :, 0:half, half:] = jnp.zeros((size, half, half), BF16)
            bands[image, part, :, half:, 0:half] = jnp.zeros((size, half, half), BF16)

    def fill(a, carry):
        def place(rows, cols, shift, spots):
            diff = (
                lax.broadcasted_iota(jnp.int32, (rows, cols), 0)
                - lax.broadcasted_iota(jnp.int32, (rows, cols), 1)
                + shift
            )
            value = jnp.zeros((rows, cols), F32)
            for b in range(size):
                value = jnp.where(diff == b - radius, psf_ref[a, b], value)
            for image in range(2):
                full = value if image == 0 else value * value
                high = full.astype(BF16)
                low = (full - high.astype(F32)).astype(BF16)
                for row, col in spots:
                    bands[image, 0, a, row : row + rows, col : col + cols] = high
                    bands[image, 1, a, row : row + rows, col : col + cols] = low

        place(half, half, 0, ((0, 0), (half, half)))
        place(16, half, -16, ((half - 16, half),))
        place(16, half, half, ((half, 0),))
        return carry

    lax.fori_loop(0, size, fill, 0)


def kernel(
    sky_count,
    psf_ref,
    off_ref,
    sci_hbm,
    inv_hbm,
    out_ref,
    sci_ref,
    inv_ref,
    raw,
    high,
    low,
    bands,
    images,
    part_send,
    part_own,
    part_recv,
    x_recv,
    load_sems,
    raw_send_sem,
    raw_recv_sem,
    core_send_sem,
    core_recv_sem,
    x_send_sem,
    x_recv_sem,
):
    visits, rows, cols = sci_ref.shape
    size = psf_ref.shape[0]
    radius = size // 2
    halo = radius + MAXOFF * BR
    blocks = rows // BR
    velocities = off_ref.shape[0]
    sky = lax.axis_index("sky")
    me = lax.axis_index("visit")
    far, near = lax.div(me, 2), lax.rem(me, 2)
    mate = (sky, 2 * far + 1 - near)
    across = (sky, 2 * (1 - far) + near)
    above, below = (sky - 1, me), (sky + 1, me)
    has_above, has_below = sky > 0, sky < sky_count - 1

    load_sci = pltpu.make_async_copy(sci_hbm, sci_ref, load_sems.at[0])
    load_inv = pltpu.make_async_copy(inv_hbm, inv_ref, load_sems.at[1])
    load_sci.start()
    load_inv.start()

    barrier = pltpu.get_barrier_semaphore()
    pl.semaphore_signal(barrier, inc=1, device_id=mate, device_id_type=MESH)
    pl.semaphore_signal(barrier, inc=1, device_id=across, device_id_type=MESH)

    @pl.when(has_above)
    def _():
        pl.semaphore_signal(barrier, inc=1, device_id=above, device_id_type=MESH)

    @pl.when(has_below)
    def _():
        pl.semaphore_signal(barrier, inc=1, device_id=below, device_id_type=MESH)

    def turn(first, count):
        def block(i, carry):
            at = pl.multiple_of(i * BR, BR)
            variance = inv_ref[:, pl.ds(at, BR), :]
            weighted = sci_ref[:, pl.ds(at, BR), :] * variance
            raw[0, pl.ds(halo + at, BR)] = jnp.swapaxes(weighted, 0, 1)
            raw[1, pl.ds(halo + at, BR)] = jnp.swapaxes(variance, 0, 1)
            return carry

        lax.fori_loop(first, first + count, block, 0)

    def remote(src, dst, send_sem, recv_sem, device):
        return pltpu.make_async_remote_copy(
            src_ref=src,
            dst_ref=dst,
            send_sem=send_sem,
            recv_sem=recv_sem,
            device_id=device,
            device_id_type=MESH,
        )

    def raw_copy(way, chunk, source, target, count, device):
        return remote(
            raw.at[:, source : source + count],
            raw.at[:, target : target + count],
            raw_send_sem.at[way, chunk],
            raw_recv_sem.at[way, chunk],
            device,
        )

    inner = halo - BR
    up = [
        raw_copy(0, 0, halo, halo + rows, inner, above),
        raw_copy(0, 1, halo + inner, halo + rows + inner, BR, above),
    ]
    down = [
        raw_copy(1, 0, halo + rows - inner, BR, inner, below),
        raw_copy(1, 1, rows, 0, BR, below),
    ]
    edge_blocks = (halo + BR - 1) // BR

    load_sci.wait()
    load_inv.wait()
    turn(0, edge_blocks)
    turn(blocks - edge_blocks, edge_blocks)
    pl.semaphore_wait(barrier, 2 + has_above.astype(jnp.int32) + has_below.astype(jnp.int32))

    for chunk in range(2):

        @pl.when(has_above)
        def _():
            up[chunk].start()

        @pl.when(has_below)
        def _():
            down[chunk].start()

    @pl.when(jnp.logical_not(has_above))
    def _():
        raw[:, 0:halo] = jnp.zeros((2, halo, visits, cols), F32)

    @pl.when(jnp.logical_not(has_below))
    def _():
        raw[:, halo + rows :] = jnp.zeros((2, halo, visits, cols), F32)

    turn(edge_blocks, blocks - 2 * edge_blocks)
    build_bands(psf_ref, size, size, bands)

    def split(odd, first, last):
        def pair_of(i, carry):
            for image in range(2):
                pair = raw[image, pl.ds(2 * i + odd, 2)].reshape(2 * visits, cols)
                head = pair.astype(BF16)
                high[image, odd, i] = head
                low[image, odd, i] = (pair - head.astype(F32)).astype(BF16)
            return carry

        lax.fori_loop(first, last, pair_of, 0)

    def correlate(starts, count):
        def image_of(image, carry):
            total = jnp.zeros((len(starts) * count * visits, cols), F32)
            for a in range(size):

                def rows_of(terms):
                    pieces = [
                        terms[image, a % 2, (start + a) // 2 : (start + a) // 2 + count // 2].reshape(
                            count * visits, cols
                        )
                        for start in starts
                    ]
                    return pieces[0] if len(pieces) == 1 else jnp.concatenate(pieces, axis=0)

                x_high, x_low = rows_of(high), rows_of(low)
                w_high, w_low = bands[image, 0, a], bands[image, 1, a]
                total = total + jnp.dot(x_high, w_high, preferred_element_type=F32)
                total = total + jnp.dot(x_low, w_high, preferred_element_type=F32)
                total = total + jnp.dot(x_high, w_low, preferred_element_type=F32)
            value = jnp.swapaxes(total.reshape(len(starts) * count, visits, cols), 0, 1)
            value = value.reshape(visits, len(starts) * count // BR, BR, cols)
            many = count // BR
            for i, start in enumerate(starts):
                images[image, :, start // BR : start // BR + many] = value[:, i * many : (i + 1) * many]
            return carry

        lax.fori_loop(0, 2, image_of, 0)

    def stack(block, target):
        def velocity(k, carry):
            totals = [None, None]
            for t in range(visits):
                place = block + MAXOFF + off_ref[k, me * visits + t]
                for image in range(2):
                    term = images[image, t, place]
                    totals[image] = term if t == 0 else totals[image] + term
            target[0, k] = totals[0]
            target[1, k] = totals[1]
            return carry

        lax.fori_loop(0, velocities, velocity, 0)

    core = [
        remote(
            part_send.at[stage],
            part_recv.at[stage],
            core_send_sem.at[stage],
            core_recv_sem.at[stage],
            mate,
        )
        for stage in range(4)
    ]
    hop = [
        remote(
            part_own.at[stage],
            x_recv.at[stage % 2],
            x_send_sem.at[stage % 2],
            x_recv_sem.at[stage % 2],
            across,
        )
        for stage in range(4)
    ]
    middle, last = blocks // 2, blocks - 1
    mine = [
        middle - near,
        middle + 1 - 3 * near,
        1 + (last - 2) * near,
        last * near,
    ]
    other = [last - block for block in mine]
    early_goes = far == near

    def give(stage):
        stack(other[stage], part_send.at[stage])
        core[stage].start()

    def keep(stage):
        stack(mine[stage], part_own.at[stage])

    def gather(stage):
        core[stage].wait_recv()

        def add(k, carry):
            for image in range(2):
                part_own[stage, image, k] += part_recv[stage, image, k]
            return carry

        lax.fori_loop(0, velocities, add, 0)

        @pl.when(early_goes if stage < 2 else jnp.logical_not(early_goes))
        def _():
            hop[stage].start()

    def arrived(chunk):
        @pl.when(has_above)
        def _():
            down[chunk].wait_recv()

        @pl.when(has_below)
        def _():
            up[chunk].wait_recv()

    def outside(block):
        @pl.when(jnp.logical_not(has_above))
        def _():
            images[:, :, block] = jnp.zeros((2, visits, BR, cols), F32)

        @pl.when(jnp.logical_not(has_below))
        def _():
            images[:, :, blocks + 2 * MAXOFF - 1 - block] = jnp.zeros((2, visits, BR, cols), F32)

    depth = rows + 2 * halo
    total_blocks = blocks + 2 * MAXOFF
    lead = 3 * BR
    lo, hi = lead // 2, (depth - lead) // 2
    split(0, lo, hi)
    split(1, lo, hi)
    correlate((lead,), rows + 2 * MAXOFF * BR - 2 * lead)
    give(0)
    keep(0)
    gather(0)

    arrived(0)
    lo1, hi1 = BR // 2, (depth - BR) // 2
    split(0, lo1, lo)
    split(1, lo1, lo)
    split(0, hi, hi1)
    split(1, hi, hi1 - 1)
    correlate((BR, (total_blocks - 3) * BR), 2 * BR)
    outside(1)
    give(1)
    give(2)
    keep(1)
    gather(1)
    keep(2)
    gather(2)

    arrived(1)
    split(0, 0, lo1)
    split(1, 0, lo1)
    split(0, hi1, depth // 2)
    split(1, hi1 - 1, depth // 2 - 1)
    correlate((0, (total_blocks - 1) * BR), BR)
    outside(0)
    give(3)
    keep(3)
    gather(3)

    def finish(stage, place):
        hop[stage].wait_recv()

        def velocity(k, carry):
            top = part_own[stage, 0, k] + x_recv[stage % 2, 0, k]
            bottom = part_own[stage, 1, k] + x_recv[stage % 2, 1, k]
            out_ref[k, place] = top / jnp.sqrt(bottom)
            return carry

        lax.fori_loop(0, velocities, velocity, 0)

    @pl.when(early_goes)
    def _():
        finish(2, 1 - near)
        finish(3, near)

    @pl.when(jnp.logical_not(early_goes))
    def _():
        finish(0, near)
        finish(1, 1 - near)

    for chunk in range(2):

        @pl.when(has_above)
        def _():
            up[chunk].wait_send()

        @pl.when(has_below)
        def _():
            down[chunk].wait_send()

    for stage in range(4):
        core[stage].wait_send()
    hop[0].wait_send()
    hop[1].wait_send()


def solution(mesh):
    sky_count = mesh.shape["sky"]

    def shards(science, inv_variance, psf_kernel, offsets):
        visits, rows, cols = science.shape
        size = psf_kernel.shape[0]
        velocities = offsets.shape[1]
        group = rows // 4
        depth = rows + 2 * (size // 2 + MAXOFF * BR)
        hbm = pl.BlockSpec(memory_space=pltpu.HBM)
        vmem = pl.BlockSpec(memory_space=pltpu.VMEM)
        smem = pl.BlockSpec(memory_space=pltpu.SMEM)
        parts = (4, 2, velocities, BR, cols)
        dma = pltpu.SemaphoreType.DMA

        def body(*refs):
            kernel(sky_count, *refs)

        stacked = pl.pallas_call(
            body,
            out_shape=jax.ShapeDtypeStruct((velocities, group // BR, BR, cols), F32),
            in_specs=[smem, smem, hbm, hbm],
            out_specs=vmem,
            scratch_shapes=[
                pltpu.VMEM((visits, rows, cols), F32),
                pltpu.VMEM((visits, rows, cols), F32),
                pltpu.VMEM((2, depth, visits, cols), F32),
                pltpu.VMEM((2, 2, depth // 2, 2 * visits, cols), BF16),
                pltpu.VMEM((2, 2, depth // 2, 2 * visits, cols), BF16),
                pltpu.VMEM((2, 2, size, cols, cols), BF16),
                pltpu.VMEM((2, visits, rows // BR + 2 * MAXOFF, BR, cols), F32),
                pltpu.VMEM(parts, F32),
                pltpu.VMEM(parts, F32),
                pltpu.VMEM(parts, F32),
                pltpu.VMEM((2,) + parts[1:], F32),
                dma((2,)),
                dma((2, 2)),
                dma((2, 2)),
                dma((4,)),
                dma((4,)),
                dma((2,)),
                dma((2,)),
            ],
            compiler_params=pltpu.CompilerParams(
                collective_id=0, has_side_effects=True, vmem_limit_bytes=63 * 1024 * 1024
            ),
        )(psf_kernel, offsets.T, science, inv_variance)
        return stacked.reshape(velocities, group, cols)

    return jax.shard_map(
        shards,
        mesh=mesh,
        in_specs=(P("visit", "sky", None), P("visit", "sky", None), P(), P()),
        out_specs=P(None, ("sky", "visit"), None),
        check_vma=False,
    )
```

```python
import jax
import jax.numpy as jnp
from jax import lax
from jax.experimental import pallas as pl
from jax.experimental.pallas import tpu as pltpu
from jax.sharding import PartitionSpec as P

BR = 8
MAXOFF = 2
MESH = pl.DeviceIdType.MESH
F32 = jnp.float32
BF16 = jnp.bfloat16


def build_bands(psf_ref, taps, size, bands):
    radius = size // 2
    half = 128
    for image in range(2):
        for part in range(2):
            bands[image, part, :, 0:half, half:] = jnp.zeros((size, half, half), BF16)
            bands[image, part, :, half:, 0:half] = jnp.zeros((size, half, half), BF16)

    def fill(a, carry):
        def place(rows, cols, shift, spots):
            diff = (
                lax.broadcasted_iota(jnp.int32, (rows, cols), 0)
                - lax.broadcasted_iota(jnp.int32, (rows, cols), 1)
                + shift
            )
            value = jnp.zeros((rows, cols), F32)
            for b in range(size):
                value = jnp.where(diff == b - radius, psf_ref[a, b], value)
            for image in range(2):
                full = value if image == 0 else value * value
                high = full.astype(BF16)
                low = (full - high.astype(F32)).astype(BF16)
                for row, col in spots:
                    bands[image, 0, a, row : row + rows, col : col + cols] = high
                    bands[image, 1, a, row : row + rows, col : col + cols] = low

        place(half, half, 0, ((0, 0), (half, half)))
        place(16, half, -16, ((half - 16, half),))
        place(16, half, half, ((half, 0),))
        return carry

    lax.fori_loop(0, size, fill, 0)


def kernel(
    sky_count,
    psf_ref,
    off_ref,
    sci_hbm,
    inv_hbm,
    out_ref,
    sci_ref,
    inv_ref,
    raw,
    high,
    low,
    bands,
    images,
    outer,
    part_send,
    part_own,
    part_recv,
    x_recv,
    load_sems,
    raw_send_sem,
    raw_recv_sem,
    core_send_sem,
    core_recv_sem,
    x_send_sem,
    x_recv_sem,
):
    visits, rows, cols = sci_ref.shape
    size = psf_ref.shape[0]
    radius = size // 2
    halo = radius + BR
    blocks = rows // BR
    velocities = off_ref.shape[0]
    sky = lax.axis_index("sky")
    me = lax.axis_index("visit")
    far, near = lax.div(me, 2), lax.rem(me, 2)
    mate = (sky, 2 * far + 1 - near)
    across = (sky, 2 * (1 - far) + near)
    above, below = (sky - 1, me), (sky + 1, me)
    has_above, has_below = sky > 0, sky < sky_count - 1

    load_sci = pltpu.make_async_copy(sci_hbm, sci_ref, load_sems.at[0])
    load_inv = pltpu.make_async_copy(inv_hbm, inv_ref, load_sems.at[1])
    load_sci.start()
    load_inv.start()

    barrier = pltpu.get_barrier_semaphore()
    pl.semaphore_signal(barrier, inc=1, device_id=mate, device_id_type=MESH)
    pl.semaphore_signal(barrier, inc=1, device_id=across, device_id_type=MESH)

    @pl.when(has_above)
    def _():
        pl.semaphore_signal(barrier, inc=1, device_id=above, device_id_type=MESH)

    @pl.when(has_below)
    def _():
        pl.semaphore_signal(barrier, inc=1, device_id=below, device_id_type=MESH)

    def turn(first, count):
        def block(i, carry):
            at = pl.multiple_of(i * BR, BR)
            variance = inv_ref[:, pl.ds(at, BR), :]
            weighted = sci_ref[:, pl.ds(at, BR), :] * variance
            raw[0, pl.ds(halo + at, BR)] = jnp.swapaxes(weighted, 0, 1)
            raw[1, pl.ds(halo + at, BR)] = jnp.swapaxes(variance, 0, 1)
            return carry

        lax.fori_loop(first, first + count, block, 0)

    def remote(src, dst, send_sem, recv_sem, device):
        return pltpu.make_async_remote_copy(
            src_ref=src,
            dst_ref=dst,
            send_sem=send_sem,
            recv_sem=recv_sem,
            device_id=device,
            device_id_type=MESH,
        )

    up = [
        remote(
            raw.at[:, halo : 2 * halo],
            raw.at[:, halo + rows :],
            raw_send_sem.at[0, 0],
            raw_recv_sem.at[0, 0],
            above,
        ),
        remote(
            images.at[:, :, MAXOFF + 1],
            outer.at[1],
            raw_send_sem.at[0, 1],
            raw_recv_sem.at[0, 1],
            above,
        ),
    ]
    down = [
        remote(
            raw.at[:, rows : rows + halo],
            raw.at[:, 0:halo],
            raw_send_sem.at[1, 0],
            raw_recv_sem.at[1, 0],
            below,
        ),
        remote(
            images.at[:, :, MAXOFF + blocks - 2],
            outer.at[0],
            raw_send_sem.at[1, 1],
            raw_recv_sem.at[1, 1],
            below,
        ),
    ]
    edge_blocks = (halo + BR - 1) // BR

    def depart(chunk):
        @pl.when(has_above)
        def _():
            up[chunk].start()

        @pl.when(has_below)
        def _():
            down[chunk].start()

    load_sci.wait()
    load_inv.wait()
    turn(0, edge_blocks)
    turn(blocks - edge_blocks, edge_blocks)
    pl.semaphore_wait(barrier, 2 + has_above.astype(jnp.int32) + has_below.astype(jnp.int32))

    depart(0)

    @pl.when(jnp.logical_not(has_above))
    def _():
        raw[:, 0:halo] = jnp.zeros((2, halo, visits, cols), F32)

    @pl.when(jnp.logical_not(has_below))
    def _():
        raw[:, halo + rows :] = jnp.zeros((2, halo, visits, cols), F32)

    turn(edge_blocks, blocks - 2 * edge_blocks)
    build_bands(psf_ref, size, size, bands)

    def split(odd, first, last):
        def pair_of(i, carry):
            for image in range(2):
                pair = raw[image, pl.ds(2 * i + odd, 2)].reshape(2 * visits, cols)
                head = pair.astype(BF16)
                high[image, odd, i] = head
                low[image, odd, i] = (pair - head.astype(F32)).astype(BF16)
            return carry

        lax.fori_loop(first, last, pair_of, 0)

    def correlate(starts, count):
        def image_of(image, carry):
            total = jnp.zeros((len(starts) * count * visits, cols), F32)
            for a in range(size):

                def rows_of(terms):
                    pieces = [
                        terms[image, a % 2, (start + a) // 2 : (start + a) // 2 + count // 2].reshape(
                            count * visits, cols
                        )
                        for start in starts
                    ]
                    return pieces[0] if len(pieces) == 1 else jnp.concatenate(pieces, axis=0)

                x_high, x_low = rows_of(high), rows_of(low)
                w_high, w_low = bands[image, 0, a], bands[image, 1, a]
                total = total + jnp.dot(x_high, w_high, preferred_element_type=F32)
                total = total + jnp.dot(x_low, w_high, preferred_element_type=F32)
                total = total + jnp.dot(x_high, w_low, preferred_element_type=F32)
            value = jnp.swapaxes(total.reshape(len(starts) * count, visits, cols), 0, 1)
            value = value.reshape(visits, len(starts) * count // BR, BR, cols)
            many = count // BR
            for i, start in enumerate(starts):
                images[image, :, 1 + start // BR : 1 + start // BR + many] = value[:, i * many : (i + 1) * many]
            return carry

        lax.fori_loop(0, 2, image_of, 0)

    def stack(block, target):
        def velocity(k, carry):
            totals = [None, None]
            for t in range(visits):
                place = block + MAXOFF + off_ref[k, me * visits + t]
                for image in range(2):
                    term = images[image, t, place]
                    totals[image] = term if t == 0 else totals[image] + term
            target[0, k] = totals[0]
            target[1, k] = totals[1]
            return carry

        lax.fori_loop(0, velocities, velocity, 0)

    core = [
        remote(
            part_send.at[stage],
            part_recv.at[stage],
            core_send_sem.at[stage],
            core_recv_sem.at[stage],
            mate,
        )
        for stage in range(4)
    ]
    hop = [
        remote(
            part_own.at[stage],
            x_recv.at[stage % 2],
            x_send_sem.at[stage % 2],
            x_recv_sem.at[stage % 2],
            across,
        )
        for stage in range(4)
    ]
    middle, last = blocks // 2, blocks - 1
    mine = [
        middle - near,
        middle + 1 - 3 * near,
        1 + (last - 2) * near,
        last * near,
    ]
    other = [last - block for block in mine]
    early_goes = far == near

    def give(stage):
        stack(other[stage], part_send.at[stage])
        core[stage].start()

    def keep(stage):
        stack(mine[stage], part_own.at[stage])

    def gather(stage):
        core[stage].wait_recv()

        def add(k, carry):
            for image in range(2):
                part_own[stage, image, k] += part_recv[stage, image, k]
            return carry

        lax.fori_loop(0, velocities, add, 0)

        @pl.when(early_goes if stage < 2 else jnp.logical_not(early_goes))
        def _():
            hop[stage].start()

    def arrived(chunk):
        @pl.when(has_above)
        def _():
            down[chunk].wait_recv()

        @pl.when(has_below)
        def _():
            up[chunk].wait_recv()

    def outside(block):
        @pl.when(jnp.logical_not(has_above))
        def _():
            images[:, :, block] = jnp.zeros((2, visits, BR, cols), F32)

        @pl.when(jnp.logical_not(has_below))
        def _():
            images[:, :, blocks + 2 * MAXOFF - 1 - block] = jnp.zeros((2, visits, BR, cols), F32)

    depth = rows + 2 * halo
    lead = 2 * BR
    lo, hi = lead // 2, (depth - lead) // 2
    split(0, lo, hi)
    split(1, lo, hi)
    correlate((lead,), rows + 2 * BR - 2 * lead)
    depart(1)
    give(0)
    keep(0)
    gather(0)

    arrived(0)
    split(0, 0, lo)
    split(1, 0, lo)
    split(0, hi, depth // 2)
    split(1, hi, depth // 2 - 1)
    correlate((0, rows), lead)
    outside(1)
    give(1)
    give(2)
    keep(1)
    gather(1)
    keep(2)
    gather(2)

    arrived(1)

    @pl.when(has_above)
    def _():
        images[:, :, 0] = outer[0]

    @pl.when(has_below)
    def _():
        images[:, :, blocks + 2 * MAXOFF - 1] = outer[1]

    outside(0)
    give(3)
    keep(3)
    gather(3)

    def finish(stage, place):
        hop[stage].wait_recv()

        def velocity(k, carry):
            top = part_own[stage, 0, k] + x_recv[stage % 2, 0, k]
            bottom = part_own[stage, 1, k] + x_recv[stage % 2, 1, k]
            out_ref[k, place] = top / jnp.sqrt(bottom)
            return carry

        lax.fori_loop(0, velocities, velocity, 0)

    @pl.when(early_goes)
    def _():
        finish(2, 1 - near)
        finish(3, near)

    @pl.when(jnp.logical_not(early_goes))
    def _():
        finish(0, near)
        finish(1, 1 - near)

    for chunk in range(2):

        @pl.when(has_above)
        def _():
            up[chunk].wait_send()

        @pl.when(has_below)
        def _():
            down[chunk].wait_send()

    for stage in range(4):
        core[stage].wait_send()
    hop[0].wait_send()
    hop[1].wait_send()


def solution(mesh):
    sky_count = mesh.shape["sky"]

    def shards(science, inv_variance, psf_kernel, offsets):
        visits, rows, cols = science.shape
        size = psf_kernel.shape[0]
        velocities = offsets.shape[1]
        group = rows // 4
        depth = rows + 2 * (size // 2 + BR)
        hbm = pl.BlockSpec(memory_space=pltpu.HBM)
        vmem = pl.BlockSpec(memory_space=pltpu.VMEM)
        smem = pl.BlockSpec(memory_space=pltpu.SMEM)
        parts = (4, 2, velocities, BR, cols)
        dma = pltpu.SemaphoreType.DMA

        def body(*refs):
            kernel(sky_count, *refs)

        stacked = pl.pallas_call(
            body,
            out_shape=jax.ShapeDtypeStruct((velocities, group // BR, BR, cols), F32),
            in_specs=[smem, smem, hbm, hbm],
            out_specs=vmem,
            scratch_shapes=[
                pltpu.VMEM((visits, rows, cols), F32),
                pltpu.VMEM((visits, rows, cols), F32),
                pltpu.VMEM((2, depth, visits, cols), F32),
                pltpu.VMEM((2, 2, depth // 2, 2 * visits, cols), BF16),
                pltpu.VMEM((2, 2, depth // 2, 2 * visits, cols), BF16),
                pltpu.VMEM((2, 2, size, cols, cols), BF16),
                pltpu.VMEM((2, visits, rows // BR + 2 * MAXOFF, BR, cols), F32),
                pltpu.VMEM((2, 2, visits, BR, cols), F32),
                pltpu.VMEM(parts, F32),
                pltpu.VMEM(parts, F32),
                pltpu.VMEM(parts, F32),
                pltpu.VMEM((2,) + parts[1:], F32),
                dma((2,)),
                dma((2, 2)),
                dma((2, 2)),
                dma((4,)),
                dma((4,)),
                dma((2,)),
                dma((2,)),
            ],
            compiler_params=pltpu.CompilerParams(
                collective_id=0, has_side_effects=True, vmem_limit_bytes=63 * 1024 * 1024
            ),
        )(psf_kernel, offsets.T, science, inv_variance)
        return stacked.reshape(velocities, group, cols)

    return jax.shard_map(
        shards,
        mesh=mesh,
        in_specs=(P("visit", "sky", None), P("visit", "sky", None), P(), P()),
        out_specs=P(None, ("sky", "visit"), None),
        check_vma=False,
    )
```

```python
import jax
import jax.numpy as jnp
from jax import lax
from jax.experimental import pallas as pl
from jax.experimental.pallas import tpu as pltpu
from jax.sharding import PartitionSpec as P

BR = 8
MAXOFF = 2
MESH = pl.DeviceIdType.MESH
F32 = jnp.float32
BF16 = jnp.bfloat16


def build_bands(psf_ref, taps, size, bands):
    radius = size // 2
    half = 128
    for image in range(2):
        for part in range(2):
            bands[image, part, :, 0:half, half:] = jnp.zeros((size, half, half), BF16)
            bands[image, part, :, half:, 0:half] = jnp.zeros((size, half, half), BF16)

    def fill(a, carry):
        def place(rows, cols, shift, spots):
            diff = (
                lax.broadcasted_iota(jnp.int32, (rows, cols), 0)
                - lax.broadcasted_iota(jnp.int32, (rows, cols), 1)
                + shift
            )
            value = jnp.zeros((rows, cols), F32)
            for b in range(size):
                value = jnp.where(diff == b - radius, psf_ref[a, b], value)
            for image in range(2):
                full = value if image == 0 else value * value
                high = full.astype(BF16)
                low = (full - high.astype(F32)).astype(BF16)
                for row, col in spots:
                    bands[image, 0, a, row : row + rows, col : col + cols] = high
                    bands[image, 1, a, row : row + rows, col : col + cols] = low

        place(half, half, 0, ((0, 0), (half, half)))
        place(16, half, -16, ((half - 16, half),))
        place(16, half, half, ((half, 0),))
        return carry

    lax.fori_loop(0, size, fill, 0)


def kernel(
    sky_count,
    psf_ref,
    off_ref,
    sci_hbm,
    inv_hbm,
    out_ref,
    sci_ref,
    inv_ref,
    raw,
    high,
    low,
    bands,
    images,
    outer,
    part_send,
    part_own,
    part_recv,
    x_recv,
    load_sems,
    raw_send_sem,
    raw_recv_sem,
    core_send_sem,
    core_recv_sem,
    x_send_sem,
    x_recv_sem,
):
    visits, rows, cols = sci_ref.shape
    size = psf_ref.shape[0]
    radius = size // 2
    halo = radius + BR
    blocks = rows // BR
    velocities = off_ref.shape[0]
    sky = lax.axis_index("sky")
    me = lax.axis_index("visit")
    far, near = lax.div(me, 2), lax.rem(me, 2)
    mate = (sky, 2 * far + 1 - near)
    across = (sky, 2 * (1 - far) + near)
    above, below = (sky - 1, me), (sky + 1, me)
    has_above, has_below = sky > 0, sky < sky_count - 1

    load_sci = pltpu.make_async_copy(sci_hbm, sci_ref, load_sems.at[0])
    load_inv = pltpu.make_async_copy(inv_hbm, inv_ref, load_sems.at[1])
    load_sci.start()
    load_inv.start()

    barrier = pltpu.get_barrier_semaphore()
    pl.semaphore_signal(barrier, inc=1, device_id=mate, device_id_type=MESH)
    pl.semaphore_signal(barrier, inc=1, device_id=across, device_id_type=MESH)

    @pl.when(has_above)
    def _():
        pl.semaphore_signal(barrier, inc=1, device_id=above, device_id_type=MESH)

    @pl.when(has_below)
    def _():
        pl.semaphore_signal(barrier, inc=1, device_id=below, device_id_type=MESH)

    def turn(first, count):
        def block(i, carry):
            at = pl.multiple_of(i * BR, BR)
            variance = inv_ref[:, pl.ds(at, BR), :]
            weighted = sci_ref[:, pl.ds(at, BR), :] * variance
            raw[0, pl.ds(halo + at, BR)] = jnp.swapaxes(weighted, 0, 1)
            raw[1, pl.ds(halo + at, BR)] = jnp.swapaxes(variance, 0, 1)
            return carry

        lax.fori_loop(first, first + count, block, 0)

    def remote(src, dst, send_sem, recv_sem, device):
        return pltpu.make_async_remote_copy(
            src_ref=src,
            dst_ref=dst,
            send_sem=send_sem,
            recv_sem=recv_sem,
            device_id=device,
            device_id_type=MESH,
        )

    up = [
        remote(
            raw.at[:, halo : 2 * halo],
            raw.at[:, halo + rows :],
            raw_send_sem.at[0, 0],
            raw_recv_sem.at[0, 0],
            above,
        ),
        remote(
            images.at[:, :, MAXOFF + 1],
            outer.at[1],
            raw_send_sem.at[0, 1],
            raw_recv_sem.at[0, 1],
            above,
        ),
    ]
    down = [
        remote(
            raw.at[:, rows : rows + halo],
            raw.at[:, 0:halo],
            raw_send_sem.at[1, 0],
            raw_recv_sem.at[1, 0],
            below,
        ),
        remote(
            images.at[:, :, MAXOFF + blocks - 2],
            outer.at[0],
            raw_send_sem.at[1, 1],
            raw_recv_sem.at[1, 1],
            below,
        ),
    ]
    edge_blocks = (halo + BR - 1) // BR

    def depart(chunk):
        @pl.when(has_above)
        def _():
            up[chunk].start()

        @pl.when(has_below)
        def _():
            down[chunk].start()

    load_sci.wait()
    load_inv.wait()
    turn(0, edge_blocks)
    turn(blocks - edge_blocks, edge_blocks)
    pl.semaphore_wait(barrier, 2 + has_above.astype(jnp.int32) + has_below.astype(jnp.int32))

    depart(0)

    @pl.when(jnp.logical_not(has_above))
    def _():
        raw[:, 0:halo] = jnp.zeros((2, halo, visits, cols), F32)

    @pl.when(jnp.logical_not(has_below))
    def _():
        raw[:, halo + rows :] = jnp.zeros((2, halo, visits, cols), F32)

    turn(edge_blocks, blocks - 2 * edge_blocks)
    build_bands(psf_ref, size, size, bands)

    def split(odd, first, last):
        def pairs_of(first, count):
            for image in range(2):
                rows_in = raw[image, pl.ds(2 * first + odd, 2 * count)]
                pairs = rows_in.reshape(count, 2 * visits, cols)
                head = pairs.astype(BF16)
                high[image, odd, pl.ds(first, count)] = head
                low[image, odd, pl.ds(first, count)] = (pairs - head.astype(F32)).astype(BF16)

        step = 4

        def several(i, carry):
            pairs_of(first + step * i, step)
            return carry

        steps = (last - first) // step
        lax.fori_loop(0, steps, several, 0)
        if first + step * steps < last:
            pairs_of(first + step * steps, last - first - step * steps)

    def correlate(starts, count):
        def image_of(image, carry):
            total = jnp.zeros((len(starts) * count * visits, cols), F32)
            for a in range(size):

                def rows_of(terms):
                    pieces = [
                        terms[image, a % 2, (start + a) // 2 : (start + a) // 2 + count // 2].reshape(
                            count * visits, cols
                        )
                        for start in starts
                    ]
                    return pieces[0] if len(pieces) == 1 else jnp.concatenate(pieces, axis=0)

                x_high, x_low = rows_of(high), rows_of(low)
                w_high, w_low = bands[image, 0, a], bands[image, 1, a]
                total = total + jnp.dot(x_high, w_high, preferred_element_type=F32)
                total = total + jnp.dot(x_low, w_high, preferred_element_type=F32)
                total = total + jnp.dot(x_high, w_low, preferred_element_type=F32)
            value = jnp.swapaxes(total.reshape(len(starts) * count, visits, cols), 0, 1)
            value = value.reshape(visits, len(starts) * count // BR, BR, cols)
            many = count // BR
            for i, start in enumerate(starts):
                images[image, :, 1 + start // BR : 1 + start // BR + many] = value[:, i * many : (i + 1) * many]
            return carry

        lax.fori_loop(0, 2, image_of, 0)

    def stack(block, target):
        def velocity(k, carry):
            totals = [None, None]
            for t in range(visits):
                place = block + MAXOFF + off_ref[k, me * visits + t]
                for image in range(2):
                    term = images[image, t, place]
                    totals[image] = term if t == 0 else totals[image] + term
            target[0, k] = totals[0]
            target[1, k] = totals[1]
            return carry

        lax.fori_loop(0, velocities, velocity, 0, unroll=4)

    core = [
        remote(
            part_send.at[stage],
            part_recv.at[stage],
            core_send_sem.at[stage],
            core_recv_sem.at[stage],
            mate,
        )
        for stage in range(4)
    ]
    hop = [
        remote(
            part_own.at[stage],
            x_recv.at[stage % 2],
            x_send_sem.at[stage % 2],
            x_recv_sem.at[stage % 2],
            across,
        )
        for stage in range(4)
    ]
    middle, last = blocks // 2, blocks - 1
    mine = [
        middle - near,
        middle + 1 - 3 * near,
        1 + (last - 2) * near,
        last * near,
    ]
    other = [last - block for block in mine]
    early_goes = far == near

    def give(stage):
        stack(other[stage], part_send.at[stage])
        core[stage].start()

    def keep(stage):
        stack(mine[stage], part_own.at[stage])

    def gather(stage):
        core[stage].wait_recv()

        def add(k, carry):
            for image in range(2):
                part_own[stage, image, k] += part_recv[stage, image, k]
            return carry

        lax.fori_loop(0, velocities, add, 0, unroll=4)

        @pl.when(early_goes if stage < 2 else jnp.logical_not(early_goes))
        def _():
            hop[stage].start()

    def arrived(chunk):
        @pl.when(has_above)
        def _():
            down[chunk].wait_recv()

        @pl.when(has_below)
        def _():
            up[chunk].wait_recv()

    def outside(block):
        @pl.when(jnp.logical_not(has_above))
        def _():
            images[:, :, block] = jnp.zeros((2, visits, BR, cols), F32)

        @pl.when(jnp.logical_not(has_below))
        def _():
            images[:, :, blocks + 2 * MAXOFF - 1 - block] = jnp.zeros((2, visits, BR, cols), F32)

    depth = rows + 2 * halo
    lead = 2 * BR
    lo, hi = lead // 2, (depth - lead) // 2
    split(0, lo, hi)
    split(1, lo, hi)
    correlate((lead,), rows + 2 * BR - 2 * lead)
    depart(1)
    give(0)
    keep(0)

    arrived(0)
    split(0, 0, lo)
    split(1, 0, lo)
    split(0, hi, depth // 2)
    split(1, hi, depth // 2 - 1)
    correlate((0, rows), lead)
    outside(1)
    gather(0)
    give(1)
    give(2)
    keep(1)
    gather(1)
    keep(2)
    gather(2)

    arrived(1)

    @pl.when(has_above)
    def _():
        images[:, :, 0] = outer[0]

    @pl.when(has_below)
    def _():
        images[:, :, blocks + 2 * MAXOFF - 1] = outer[1]

    outside(0)
    give(3)
    keep(3)
    gather(3)

    def finish(stage, place):
        hop[stage].wait_recv()

        def velocity(k, carry):
            top = part_own[stage, 0, k] + x_recv[stage % 2, 0, k]
            bottom = part_own[stage, 1, k] + x_recv[stage % 2, 1, k]
            out_ref[k, place] = top / jnp.sqrt(bottom)
            return carry

        lax.fori_loop(0, velocities, velocity, 0, unroll=4)

    @pl.when(early_goes)
    def _():
        finish(2, 1 - near)
        finish(3, near)

    @pl.when(jnp.logical_not(early_goes))
    def _():
        finish(0, near)
        finish(1, 1 - near)

    for chunk in range(2):

        @pl.when(has_above)
        def _():
            up[chunk].wait_send()

        @pl.when(has_below)
        def _():
            down[chunk].wait_send()

    for stage in range(4):
        core[stage].wait_send()
    hop[0].wait_send()
    hop[1].wait_send()


def solution(mesh):
    sky_count = mesh.shape["sky"]

    def shards(science, inv_variance, psf_kernel, offsets):
        visits, rows, cols = science.shape
        size = psf_kernel.shape[0]
        velocities = offsets.shape[1]
        group = rows // 4
        depth = rows + 2 * (size // 2 + BR)
        hbm = pl.BlockSpec(memory_space=pltpu.HBM)
        vmem = pl.BlockSpec(memory_space=pltpu.VMEM)
        smem = pl.BlockSpec(memory_space=pltpu.SMEM)
        parts = (4, 2, velocities, BR, cols)
        dma = pltpu.SemaphoreType.DMA

        def body(*refs):
            kernel(sky_count, *refs)

        stacked = pl.pallas_call(
            body,
            out_shape=jax.ShapeDtypeStruct((velocities, group // BR, BR, cols), F32),
            in_specs=[smem, smem, hbm, hbm],
            out_specs=vmem,
            scratch_shapes=[
                pltpu.VMEM((visits, rows, cols), F32),
                pltpu.VMEM((visits, rows, cols), F32),
                pltpu.VMEM((2, depth, visits, cols), F32),
                pltpu.VMEM((2, 2, depth // 2, 2 * visits, cols), BF16),
                pltpu.VMEM((2, 2, depth // 2, 2 * visits, cols), BF16),
                pltpu.VMEM((2, 2, size, cols, cols), BF16),
                pltpu.VMEM((2, visits, rows // BR + 2 * MAXOFF, BR, cols), F32),
                pltpu.VMEM((2, 2, visits, BR, cols), F32),
                pltpu.VMEM(parts, F32),
                pltpu.VMEM(parts, F32),
                pltpu.VMEM(parts, F32),
                pltpu.VMEM((2,) + parts[1:], F32),
                dma((2,)),
                dma((2, 2)),
                dma((2, 2)),
                dma((4,)),
                dma((4,)),
                dma((2,)),
                dma((2,)),
            ],
            compiler_params=pltpu.CompilerParams(
                collective_id=0, has_side_effects=True, vmem_limit_bytes=63 * 1024 * 1024
            ),
        )(psf_kernel, offsets.T, science, inv_variance)
        return stacked.reshape(velocities, group, cols)

    return jax.shard_map(
        shards,
        mesh=mesh,
        in_specs=(P("visit", "sky", None), P("visit", "sky", None), P(), P()),
        out_specs=P(None, ("sky", "visit"), None),
        check_vma=False,
    )
```

```python
import jax
import jax.numpy as jnp
from jax import lax
from jax.experimental import pallas as pl
from jax.experimental.pallas import tpu as pltpu
from jax.sharding import PartitionSpec as P

BR = 8
MAXOFF = 2
MESH = pl.DeviceIdType.MESH
F32 = jnp.float32
BF16 = jnp.bfloat16


def build_bands(psf_ref, taps, size, bands):
    radius = size // 2
    half = 128
    for image in range(2):
        for part in range(2):
            bands[image, part, :, 0:half, half:] = jnp.zeros((size, half, half), BF16)
            bands[image, part, :, half:, 0:half] = jnp.zeros((size, half, half), BF16)

    def fill(a, carry):
        def place(rows, cols, shift, spots):
            diff = (
                lax.broadcasted_iota(jnp.int32, (rows, cols), 0)
                - lax.broadcasted_iota(jnp.int32, (rows, cols), 1)
                + shift
            )
            value = jnp.zeros((rows, cols), F32)
            for b in range(size):
                value = jnp.where(diff == b - radius, psf_ref[a, b], value)
            for image in range(2):
                full = value if image == 0 else value * value
                high = full.astype(BF16)
                low = (full - high.astype(F32)).astype(BF16)
                for row, col in spots:
                    bands[image, 0, a, row : row + rows, col : col + cols] = high
                    bands[image, 1, a, row : row + rows, col : col + cols] = low

        place(half, half, 0, ((0, 0), (half, half)))
        place(16, half, -16, ((half - 16, half),))
        place(16, half, half, ((half, 0),))
        return carry

    lax.fori_loop(0, size, fill, 0)


def kernel(
    sky_count,
    psf_ref,
    off_ref,
    sci_hbm,
    inv_hbm,
    out_ref,
    sci_ref,
    inv_ref,
    raw,
    high,
    low,
    bands,
    images,
    spill,
    part_send,
    part_own,
    part_recv,
    x_recv,
    load_sems,
    raw_send_sem,
    raw_recv_sem,
    core_send_sem,
    core_recv_sem,
    x_send_sem,
    x_recv_sem,
    spill_send_sem,
    spill_recv_sem,
):
    visits, rows, cols = sci_ref.shape
    size = psf_ref.shape[0]
    radius = size // 2
    halo = radius + BR
    blocks = rows // BR
    velocities = off_ref.shape[0]
    sky = lax.axis_index("sky")
    me = lax.axis_index("visit")
    far, near = lax.div(me, 2), lax.rem(me, 2)
    mate = (sky, 2 * far + 1 - near)
    across = (sky, 2 * (1 - far) + near)
    above, below = (sky - 1, me), (sky + 1, me)
    has_above, has_below = sky > 0, sky < sky_count - 1

    load_sci = pltpu.make_async_copy(sci_hbm, sci_ref, load_sems.at[0])
    load_inv = pltpu.make_async_copy(inv_hbm, inv_ref, load_sems.at[1])
    load_sci.start()
    load_inv.start()

    barrier = pltpu.get_barrier_semaphore()
    pl.semaphore_signal(barrier, inc=1, device_id=mate, device_id_type=MESH)
    pl.semaphore_signal(barrier, inc=1, device_id=across, device_id_type=MESH)

    @pl.when(has_above)
    def _():
        pl.semaphore_signal(barrier, inc=1, device_id=above, device_id_type=MESH)

    @pl.when(has_below)
    def _():
        pl.semaphore_signal(barrier, inc=1, device_id=below, device_id_type=MESH)

    def turn(first, count):
        def block(i, carry):
            at = pl.multiple_of(i * BR, BR)
            variance = inv_ref[:, pl.ds(at, BR), :]
            weighted = sci_ref[:, pl.ds(at, BR), :] * variance
            raw[0, pl.ds(halo + at, BR)] = jnp.swapaxes(weighted, 0, 1)
            raw[1, pl.ds(halo + at, BR)] = jnp.swapaxes(variance, 0, 1)
            return carry

        lax.fori_loop(first, first + count, block, 0)

    def remote(src, dst, send_sem, recv_sem, device):
        return pltpu.make_async_remote_copy(
            src_ref=src,
            dst_ref=dst,
            send_sem=send_sem,
            recv_sem=recv_sem,
            device_id=device,
            device_id_type=MESH,
        )

    up = [
        remote(
            raw.at[:, halo : 2 * halo],
            raw.at[:, halo + rows :],
            raw_send_sem.at[0, 0],
            raw_recv_sem.at[0, 0],
            above,
        ),
    ]
    down = [
        remote(
            raw.at[:, rows : rows + halo],
            raw.at[:, 0:halo],
            raw_send_sem.at[1, 0],
            raw_recv_sem.at[1, 0],
            below,
        ),
    ]
    edge_blocks = (halo + BR - 1) // BR

    def depart(chunk):
        @pl.when(has_above)
        def _():
            up[chunk].start()

        @pl.when(has_below)
        def _():
            down[chunk].start()

    load_sci.wait()
    load_inv.wait()
    turn(0, edge_blocks)
    turn(blocks - edge_blocks, edge_blocks)
    pl.semaphore_wait(barrier, 2 + has_above.astype(jnp.int32) + has_below.astype(jnp.int32))

    depart(0)

    @pl.when(jnp.logical_not(has_above))
    def _():
        raw[:, 0:halo] = jnp.zeros((2, halo, visits, cols), F32)

    @pl.when(jnp.logical_not(has_below))
    def _():
        raw[:, halo + rows :] = jnp.zeros((2, halo, visits, cols), F32)

    turn(edge_blocks, blocks - 2 * edge_blocks)
    build_bands(psf_ref, size, size, bands)

    def split(odd, first, last):
        def pairs_of(first, count):
            for image in range(2):
                rows_in = raw[image, pl.ds(2 * first + odd, 2 * count)]
                pairs = rows_in.reshape(count, 2 * visits, cols)
                head = pairs.astype(BF16)
                high[image, odd, pl.ds(first, count)] = head
                low[image, odd, pl.ds(first, count)] = (pairs - head.astype(F32)).astype(BF16)

        step = 4

        def several(i, carry):
            pairs_of(first + step * i, step)
            return carry

        steps = (last - first) // step
        lax.fori_loop(0, steps, several, 0)
        if first + step * steps < last:
            pairs_of(first + step * steps, last - first - step * steps)

    def correlate(starts, count):
        def image_of(image, carry):
            total = jnp.zeros((len(starts) * count * visits, cols), F32)
            for a in range(size):

                def rows_of(terms):
                    pieces = [
                        terms[image, a % 2, (start + a) // 2 : (start + a) // 2 + count // 2].reshape(
                            count * visits, cols
                        )
                        for start in starts
                    ]
                    return pieces[0] if len(pieces) == 1 else jnp.concatenate(pieces, axis=0)

                x_high, x_low = rows_of(high), rows_of(low)
                w_high, w_low = bands[image, 0, a], bands[image, 1, a]
                total = total + jnp.dot(x_high, w_high, preferred_element_type=F32)
                total = total + jnp.dot(x_low, w_high, preferred_element_type=F32)
                total = total + jnp.dot(x_high, w_low, preferred_element_type=F32)
            value = jnp.swapaxes(total.reshape(len(starts) * count, visits, cols), 0, 1)
            value = value.reshape(visits, len(starts) * count // BR, BR, cols)
            many = count // BR
            for i, start in enumerate(starts):
                images[image, :, 1 + start // BR : 1 + start // BR + many] = value[:, i * many : (i + 1) * many]
            return carry

        lax.fori_loop(0, 2, image_of, 0)

    def stack(block, target):
        def velocity(k, carry):
            totals = [None, None]
            for t in range(visits):
                place = block + MAXOFF + off_ref[k, me * visits + t]
                for image in range(2):
                    term = images[image, t, place]
                    totals[image] = term if t == 0 else totals[image] + term
            target[0, k] = totals[0]
            target[1, k] = totals[1]
            return carry

        lax.fori_loop(0, velocities, velocity, 0, unroll=4)

    core = [
        remote(
            part_send.at[stage],
            part_recv.at[stage],
            core_send_sem.at[stage],
            core_recv_sem.at[stage],
            mate,
        )
        for stage in range(4)
    ]
    hop = [
        remote(
            part_own.at[stage],
            x_recv.at[stage % 2],
            x_send_sem.at[stage % 2],
            x_recv_sem.at[stage % 2],
            across,
        )
        for stage in range(4)
    ]
    middle, last = blocks // 2, blocks - 1
    mine = [
        middle - near,
        middle + 1 - 3 * near,
        1 + (last - 2) * near,
        last * near,
    ]
    other = [last - block for block in mine]
    early_goes = far == near

    def give(stage):
        stack(other[stage], part_send.at[stage])
        core[stage].start()

    def keep(stage):
        stack(mine[stage], part_own.at[stage])

    def gather(stage):
        core[stage].wait_recv()

        def add(k, carry):
            for image in range(2):
                part_own[stage, image, k] += part_recv[stage, image, k]
            return carry

        lax.fori_loop(0, velocities, add, 0, unroll=4)

        @pl.when(early_goes if stage < 2 else jnp.logical_not(early_goes))
        def _():
            hop[stage].start()

    def spread(way, slot):
        source = MAXOFF + blocks - 2 - (blocks - 3) * way
        wanted = 2 * MAXOFF * way - MAXOFF

        def velocity(k, carry):
            totals = [None, None]
            for t in range(visits):
                place = jnp.where(off_ref[k, me * visits + t] == wanted, source, 0)
                for image in range(2):
                    term = images[image, t, place]
                    totals[image] = term if t == 0 else totals[image] + term
            spill[slot, 0, k] = totals[0]
            spill[slot, 1, k] = totals[1]
            return carry

        lax.fori_loop(0, velocities, velocity, 0, unroll=4)

    def spill_copy(src, dst, device):
        return remote(spill.at[src], spill.at[dst], spill_send_sem.at[dst - 2], spill_recv_sem.at[dst - 2], device)

    spill_core = spill_copy(0, 2, mate)
    spill_hop = spill_copy(1, 3, across)
    spill_on = spill_copy(1, 4, (sky + 1 - 2 * near, me))
    passes = jnp.logical_and(early_goes, jnp.where(near == 0, has_below, has_above))
    takes = jnp.where(near == 0, has_above, has_below)

    def arrived(chunk):
        @pl.when(has_above)
        def _():
            down[chunk].wait_recv()

        @pl.when(has_below)
        def _():
            up[chunk].wait_recv()

    def outside(block):
        @pl.when(jnp.logical_not(has_above))
        def _():
            images[:, :, block] = jnp.zeros((2, visits, BR, cols), F32)

        @pl.when(jnp.logical_not(has_below))
        def _():
            images[:, :, blocks + 2 * MAXOFF - 1 - block] = jnp.zeros((2, visits, BR, cols), F32)

    depth = rows + 2 * halo
    lead = 2 * BR
    lo, hi = lead // 2, (depth - lead) // 2
    split(0, lo, hi)
    split(1, lo, hi)
    correlate((lead,), rows + 2 * BR - 2 * lead)
    images[:, :, 0] = jnp.zeros((2, visits, BR, cols), F32)
    images[:, :, blocks + 2 * MAXOFF - 1] = jnp.zeros((2, visits, BR, cols), F32)
    spread(1 - near, 0)
    spill_core.start()
    spread(near, 1)
    give(0)
    keep(0)
    spill_core.wait_recv()

    def join(k, carry):
        for image in range(2):
            spill[1, image, k] += spill[2, image, k]
        return carry

    lax.fori_loop(0, velocities, join, 0, unroll=4)

    @pl.when(jnp.logical_not(early_goes))
    def _():
        spill_hop.start()

    arrived(0)
    split(0, 0, lo)
    split(1, 0, lo)
    split(0, hi, depth // 2)
    split(1, hi, depth // 2 - 1)
    correlate((0, rows), lead)
    outside(1)

    @pl.when(early_goes)
    def _():
        spill_hop.wait_recv()
        spill[1] += spill[3]

    @pl.when(passes)
    def _():
        spill_on.start()

    gather(0)
    give(1)
    give(2)
    keep(1)
    gather(1)
    keep(2)
    gather(2)

    give(3)
    keep(3)
    gather(3)

    def finish(stage, place):
        hop[stage].wait_recv()

        def velocity(k, carry):
            top = part_own[stage, 0, k] + x_recv[stage % 2, 0, k]
            bottom = part_own[stage, 1, k] + x_recv[stage % 2, 1, k]
            out_ref[k, place] = top / jnp.sqrt(bottom)
            return carry

        lax.fori_loop(0, velocities, velocity, 0, unroll=4)

    @pl.when(early_goes)
    def _():
        finish(2, 1 - near)

        @pl.when(takes)
        def _():
            spill_on.wait_recv()
            part_own[3] += spill[4]

        finish(3, near)

    @pl.when(jnp.logical_not(early_goes))
    def _():
        finish(0, near)
        finish(1, 1 - near)

    for chunk in range(1):

        @pl.when(has_above)
        def _():
            up[chunk].wait_send()

        @pl.when(has_below)
        def _():
            down[chunk].wait_send()

    for stage in range(4):
        core[stage].wait_send()
    hop[0].wait_send()
    hop[1].wait_send()
    spill_core.wait_send()

    @pl.when(jnp.logical_not(early_goes))
    def _():
        spill_hop.wait_send()

    @pl.when(passes)
    def _():
        spill_on.wait_send()


def solution(mesh):
    sky_count = mesh.shape["sky"]

    def shards(science, inv_variance, psf_kernel, offsets):
        visits, rows, cols = science.shape
        size = psf_kernel.shape[0]
        velocities = offsets.shape[1]
        group = rows // 4
        depth = rows + 2 * (size // 2 + BR)
        hbm = pl.BlockSpec(memory_space=pltpu.HBM)
        vmem = pl.BlockSpec(memory_space=pltpu.VMEM)
        smem = pl.BlockSpec(memory_space=pltpu.SMEM)
        parts = (4, 2, velocities, BR, cols)
        dma = pltpu.SemaphoreType.DMA

        def body(*refs):
            kernel(sky_count, *refs)

        stacked = pl.pallas_call(
            body,
            out_shape=jax.ShapeDtypeStruct((velocities, group // BR, BR, cols), F32),
            in_specs=[smem, smem, hbm, hbm],
            out_specs=vmem,
            scratch_shapes=[
                pltpu.VMEM((visits, rows, cols), F32),
                pltpu.VMEM((visits, rows, cols), F32),
                pltpu.VMEM((2, depth, visits, cols), F32),
                pltpu.VMEM((2, 2, depth // 2, 2 * visits, cols), BF16),
                pltpu.VMEM((2, 2, depth // 2, 2 * visits, cols), BF16),
                pltpu.VMEM((2, 2, size, cols, cols), BF16),
                pltpu.VMEM((2, visits, rows // BR + 2 * MAXOFF, BR, cols), F32),
                pltpu.VMEM((5,) + parts[1:], F32),
                pltpu.VMEM(parts, F32),
                pltpu.VMEM(parts, F32),
                pltpu.VMEM(parts, F32),
                pltpu.VMEM((2,) + parts[1:], F32),
                dma((2,)),
                dma((2, 2)),
                dma((2, 2)),
                dma((4,)),
                dma((4,)),
                dma((2,)),
                dma((2,)),
                dma((3,)),
                dma((3,)),
            ],
            compiler_params=pltpu.CompilerParams(
                collective_id=0, has_side_effects=True, vmem_limit_bytes=63 * 1024 * 1024
            ),
        )(psf_kernel, offsets.T, science, inv_variance)
        return stacked.reshape(velocities, group, cols)

    return jax.shard_map(
        shards,
        mesh=mesh,
        in_specs=(P("visit", "sky", None), P("visit", "sky", None), P(), P()),
        out_specs=P(None, ("sky", "visit"), None),
        check_vma=False,
    )
```

```python
import jax
import jax.numpy as jnp
from jax import lax
from jax.experimental import pallas as pl
from jax.experimental.pallas import tpu as pltpu
from jax.sharding import PartitionSpec as P

BR = 8
MAXOFF = 2
MESH = pl.DeviceIdType.MESH
F32 = jnp.float32
BF16 = jnp.bfloat16


def build_bands(psf_ref, taps, size, bands):
    radius = size // 2
    half = 128
    for image in range(2):
        for part in range(2):
            bands[image, part, :, 0:half, half:] = jnp.zeros((size, half, half), BF16)
            bands[image, part, :, half:, 0:half] = jnp.zeros((size, half, half), BF16)

    def fill(a, carry):
        def place(rows, cols, shift, spots):
            diff = (
                lax.broadcasted_iota(jnp.int32, (rows, cols), 0)
                - lax.broadcasted_iota(jnp.int32, (rows, cols), 1)
                + shift
            )
            value = jnp.zeros((rows, cols), F32)
            for b in range(size):
                value = jnp.where(diff == b - radius, psf_ref[a, b], value)
            for image in range(2):
                full = value if image == 0 else value * value
                high = full.astype(BF16)
                low = (full - high.astype(F32)).astype(BF16)
                for row, col in spots:
                    bands[image, 0, a, row : row + rows, col : col + cols] = high
                    bands[image, 1, a, row : row + rows, col : col + cols] = low

        place(half, half, 0, ((0, 0), (half, half)))
        place(16, half, -16, ((half - 16, half),))
        place(16, half, half, ((half, 0),))
        return carry

    lax.fori_loop(0, size, fill, 0)


def kernel(
    sky_count,
    psf_ref,
    off_ref,
    sci_hbm,
    inv_hbm,
    out_ref,
    sci_ref,
    inv_ref,
    raw,
    high,
    low,
    bands,
    images,
    spill,
    part_send,
    part_own,
    part_recv,
    x_recv,
    load_sems,
    raw_send_sem,
    raw_recv_sem,
    core_send_sem,
    core_recv_sem,
    x_send_sem,
    x_recv_sem,
    spill_send_sem,
    spill_recv_sem,
):
    visits, rows, cols = sci_ref.shape
    size = psf_ref.shape[0]
    radius = size // 2
    halo = radius + BR
    blocks = rows // BR
    velocities = off_ref.shape[0]
    sky = lax.axis_index("sky")
    me = lax.axis_index("visit")
    far, near = lax.div(me, 2), lax.rem(me, 2)
    mate = (sky, 2 * far + 1 - near)
    across = (sky, 2 * (1 - far) + near)
    above, below = (sky - 1, me), (sky + 1, me)
    has_above, has_below = sky > 0, sky < sky_count - 1

    load_sci = pltpu.make_async_copy(sci_hbm, sci_ref, load_sems.at[0])
    load_inv = pltpu.make_async_copy(inv_hbm, inv_ref, load_sems.at[1])
    load_sci.start()
    load_inv.start()

    barrier = pltpu.get_barrier_semaphore()
    pl.semaphore_signal(barrier, inc=1, device_id=mate, device_id_type=MESH)
    pl.semaphore_signal(barrier, inc=1, device_id=across, device_id_type=MESH)

    @pl.when(has_above)
    def _():
        pl.semaphore_signal(barrier, inc=1, device_id=above, device_id_type=MESH)

    @pl.when(has_below)
    def _():
        pl.semaphore_signal(barrier, inc=1, device_id=below, device_id_type=MESH)

    def turn(first, count):
        def block(i, carry):
            at = pl.multiple_of(i * BR, BR)
            variance = inv_ref[:, pl.ds(at, BR), :]
            weighted = sci_ref[:, pl.ds(at, BR), :] * variance
            raw[0, pl.ds(halo + at, BR)] = jnp.swapaxes(weighted, 0, 1)
            raw[1, pl.ds(halo + at, BR)] = jnp.swapaxes(variance, 0, 1)
            return carry

        lax.fori_loop(first, first + count, block, 0)

    def remote(src, dst, send_sem, recv_sem, device):
        return pltpu.make_async_remote_copy(
            src_ref=src,
            dst_ref=dst,
            send_sem=send_sem,
            recv_sem=recv_sem,
            device_id=device,
            device_id_type=MESH,
        )

    up = [
        remote(
            raw.at[:, halo : 2 * halo],
            raw.at[:, halo + rows :],
            raw_send_sem.at[0, 0],
            raw_recv_sem.at[0, 0],
            above,
        ),
    ]
    down = [
        remote(
            raw.at[:, rows : rows + halo],
            raw.at[:, 0:halo],
            raw_send_sem.at[1, 0],
            raw_recv_sem.at[1, 0],
            below,
        ),
    ]
    edge_blocks = (halo + BR - 1) // BR

    def depart(chunk):
        @pl.when(has_above)
        def _():
            up[chunk].start()

        @pl.when(has_below)
        def _():
            down[chunk].start()

    load_sci.wait()
    load_inv.wait()
    turn(0, edge_blocks)
    turn(blocks - edge_blocks, edge_blocks)
    pl.semaphore_wait(barrier, 2 + has_above.astype(jnp.int32) + has_below.astype(jnp.int32))

    depart(0)

    @pl.when(jnp.logical_not(has_above))
    def _():
        raw[:, 0:halo] = jnp.zeros((2, halo, visits, cols), F32)

    @pl.when(jnp.logical_not(has_below))
    def _():
        raw[:, halo + rows :] = jnp.zeros((2, halo, visits, cols), F32)

    turn(edge_blocks, blocks - 2 * edge_blocks)
    build_bands(psf_ref, size, size, bands)

    def split(odd, first, last):
        def pairs_of(first, count):
            for image in range(2):
                rows_in = raw[image, pl.ds(2 * first + odd, 2 * count)]
                pairs = rows_in.reshape(count, 2 * visits, cols)
                head = pairs.astype(BF16)
                high[image, odd, pl.ds(first, count)] = head
                low[image, odd, pl.ds(first, count)] = (pairs - head.astype(F32)).astype(BF16)

        step = 4

        def several(i, carry):
            pairs_of(first + step * i, step)
            return carry

        steps = (last - first) // step
        lax.fori_loop(0, steps, several, 0)
        if first + step * steps < last:
            pairs_of(first + step * steps, last - first - step * steps)

    def correlate(starts, count):
        def image_of(image, carry):
            total = jnp.zeros((len(starts) * count * visits, cols), F32)
            for a in range(size):

                def rows_of(terms):
                    pieces = [
                        terms[image, a % 2, (start + a) // 2 : (start + a) // 2 + count // 2].reshape(
                            count * visits, cols
                        )
                        for start in starts
                    ]
                    return pieces[0] if len(pieces) == 1 else jnp.concatenate(pieces, axis=0)

                x_high, x_low = rows_of(high), rows_of(low)
                w_high, w_low = bands[image, 0, a], bands[image, 1, a]
                total = total + jnp.dot(x_high, w_high, preferred_element_type=F32)
                total = total + jnp.dot(x_low, w_high, preferred_element_type=F32)
                total = total + jnp.dot(x_high, w_low, preferred_element_type=F32)
            value = jnp.swapaxes(total.reshape(len(starts) * count, visits, cols), 0, 1)
            value = value.reshape(visits, len(starts) * count // BR, BR, cols)
            many = count // BR
            for i, start in enumerate(starts):
                images[image, :, 1 + start // BR : 1 + start // BR + many] = value[:, i * many : (i + 1) * many]
            return carry

        lax.fori_loop(0, 2, image_of, 0)

    def stack(block, target):
        def velocity(k, carry):
            totals = [None, None]
            for t in range(visits):
                place = block + MAXOFF + off_ref[k, me * visits + t]
                for image in range(2):
                    term = images[image, t, place]
                    totals[image] = term if t == 0 else totals[image] + term
            target[0, k] = totals[0]
            target[1, k] = totals[1]
            return carry

        lax.fori_loop(0, velocities, velocity, 0, unroll=4)

    core = [
        remote(
            part_send.at[stage],
            part_recv.at[stage],
            core_send_sem.at[stage],
            core_recv_sem.at[stage],
            mate,
        )
        for stage in range(4)
    ]
    hop = [
        remote(
            part_own.at[stage],
            x_recv.at[stage % 2],
            x_send_sem.at[stage % 2],
            x_recv_sem.at[stage % 2],
            across,
        )
        for stage in range(4)
    ]
    middle, last = blocks // 2, blocks - 1
    mine = [
        middle - near,
        middle + 1 - 3 * near,
        1 + (last - 2) * near,
        last * near,
    ]
    other = [last - block for block in mine]
    early_goes = far == near

    def give(stage):
        stack(other[stage], part_send.at[stage])
        core[stage].start()

    def keep(stage):
        stack(mine[stage], part_own.at[stage])

    def gather(stage):
        core[stage].wait_recv()

        def add(k, carry):
            for image in range(2):
                part_own[stage, image, k] += part_recv[stage, image, k]
            return carry

        lax.fori_loop(0, velocities, add, 0, unroll=4)

        @pl.when(early_goes if stage < 2 else jnp.logical_not(early_goes))
        def _():
            hop[stage].start()

    def spread(way, slot):
        source = MAXOFF + blocks - 2 - (blocks - 3) * way
        wanted = 2 * MAXOFF * way - MAXOFF

        def velocity(k, carry):
            totals = [None, None]
            for t in range(visits):
                place = jnp.where(off_ref[k, me * visits + t] == wanted, source, 0)
                for image in range(2):
                    term = images[image, t, place]
                    totals[image] = term if t == 0 else totals[image] + term
            spill[slot, 0, k] = totals[0]
            spill[slot, 1, k] = totals[1]
            return carry

        lax.fori_loop(0, velocities, velocity, 0, unroll=4)

    def spill_copy(src, dst, device):
        return remote(spill.at[src], spill.at[dst], spill_send_sem.at[dst - 2], spill_recv_sem.at[dst - 2], device)

    spill_core = spill_copy(0, 2, mate)
    spill_hop = spill_copy(1, 3, across)
    spill_on = spill_copy(1, 4, (sky + 1 - 2 * near, me))
    passes = jnp.logical_and(early_goes, jnp.where(near == 0, has_below, has_above))
    takes = jnp.where(near == 0, has_above, has_below)

    def arrived(chunk):
        @pl.when(has_above)
        def _():
            down[chunk].wait_recv()

        @pl.when(has_below)
        def _():
            up[chunk].wait_recv()

    def outside(block):
        @pl.when(jnp.logical_not(has_above))
        def _():
            images[:, :, block] = jnp.zeros((2, visits, BR, cols), F32)

        @pl.when(jnp.logical_not(has_below))
        def _():
            images[:, :, blocks + 2 * MAXOFF - 1 - block] = jnp.zeros((2, visits, BR, cols), F32)

    depth = rows + 2 * halo
    lead = 2 * BR
    lo, hi = lead // 2, (depth - lead) // 2
    split(0, lo, hi)
    split(1, lo, hi)
    correlate((lead,), rows + 2 * BR - 2 * lead)
    images[:, :, 0] = jnp.zeros((2, visits, BR, cols), F32)
    images[:, :, blocks + 2 * MAXOFF - 1] = jnp.zeros((2, visits, BR, cols), F32)
    spread(1 - near, 0)
    spill_core.start()
    spread(near, 1)
    give(0)
    keep(0)
    spill_core.wait_recv()

    def join(k, carry):
        for image in range(2):
            spill[1, image, k] += spill[2, image, k]
        return carry

    lax.fori_loop(0, velocities, join, 0, unroll=4)

    @pl.when(jnp.logical_not(early_goes))
    def _():
        spill_hop.start()

    arrived(0)

    @pl.when(early_goes)
    def _():
        spill_hop.wait_recv()
        spill[1] += spill[3]

    @pl.when(passes)
    def _():
        spill_on.start()

    split(0, 0, lo)
    split(1, 0, lo)
    split(0, hi, depth // 2)
    split(1, hi, depth // 2 - 1)
    correlate((0, rows), lead)
    outside(1)

    gather(0)
    give(1)
    give(2)
    keep(1)
    gather(1)
    keep(2)
    gather(2)

    give(3)
    keep(3)
    gather(3)

    def finish(stage, place):
        hop[stage].wait_recv()

        def velocity(k, carry):
            top = part_own[stage, 0, k] + x_recv[stage % 2, 0, k]
            bottom = part_own[stage, 1, k] + x_recv[stage % 2, 1, k]
            out_ref[k, place] = top / jnp.sqrt(bottom)
            return carry

        lax.fori_loop(0, velocities, velocity, 0, unroll=4)

    @pl.when(early_goes)
    def _():
        finish(2, 1 - near)

        @pl.when(takes)
        def _():
            spill_on.wait_recv()
            part_own[3] += spill[4]

        finish(3, near)

    @pl.when(jnp.logical_not(early_goes))
    def _():
        finish(0, near)
        finish(1, 1 - near)

    for chunk in range(1):

        @pl.when(has_above)
        def _():
            up[chunk].wait_send()

        @pl.when(has_below)
        def _():
            down[chunk].wait_send()

    for stage in range(4):
        core[stage].wait_send()
    hop[0].wait_send()
    hop[1].wait_send()
    spill_core.wait_send()

    @pl.when(jnp.logical_not(early_goes))
    def _():
        spill_hop.wait_send()

    @pl.when(passes)
    def _():
        spill_on.wait_send()


def solution(mesh):
    sky_count = mesh.shape["sky"]

    def shards(science, inv_variance, psf_kernel, offsets):
        visits, rows, cols = science.shape
        size = psf_kernel.shape[0]
        velocities = offsets.shape[1]
        group = rows // 4
        depth = rows + 2 * (size // 2 + BR)
        hbm = pl.BlockSpec(memory_space=pltpu.HBM)
        vmem = pl.BlockSpec(memory_space=pltpu.VMEM)
        smem = pl.BlockSpec(memory_space=pltpu.SMEM)
        parts = (4, 2, velocities, BR, cols)
        dma = pltpu.SemaphoreType.DMA

        def body(*refs):
            kernel(sky_count, *refs)

        stacked = pl.pallas_call(
            body,
            out_shape=jax.ShapeDtypeStruct((velocities, group // BR, BR, cols), F32),
            in_specs=[smem, smem, hbm, hbm],
            out_specs=vmem,
            scratch_shapes=[
                pltpu.VMEM((visits, rows, cols), F32),
                pltpu.VMEM((visits, rows, cols), F32),
                pltpu.VMEM((2, depth, visits, cols), F32),
                pltpu.VMEM((2, 2, depth // 2, 2 * visits, cols), BF16),
                pltpu.VMEM((2, 2, depth // 2, 2 * visits, cols), BF16),
                pltpu.VMEM((2, 2, size, cols, cols), BF16),
                pltpu.VMEM((2, visits, rows // BR + 2 * MAXOFF, BR, cols), F32),
                pltpu.VMEM((5,) + parts[1:], F32),
                pltpu.VMEM(parts, F32),
                pltpu.VMEM(parts, F32),
                pltpu.VMEM(parts, F32),
                pltpu.VMEM((2,) + parts[1:], F32),
                dma((2,)),
                dma((2, 2)),
                dma((2, 2)),
                dma((4,)),
                dma((4,)),
                dma((2,)),
                dma((2,)),
                dma((3,)),
                dma((3,)),
            ],
            compiler_params=pltpu.CompilerParams(
                collective_id=0, has_side_effects=True, vmem_limit_bytes=63 * 1024 * 1024
            ),
        )(psf_kernel, offsets.T, science, inv_variance)
        return stacked.reshape(velocities, group, cols)

    return jax.shard_map(
        shards,
        mesh=mesh,
        in_specs=(P("visit", "sky", None), P("visit", "sky", None), P(), P()),
        out_specs=P(None, ("sky", "visit"), None),
        check_vma=False,
    )
```

```python
import jax
import jax.numpy as jnp
from jax import lax
from jax.experimental import pallas as pl
from jax.experimental.pallas import tpu as pltpu
from jax.sharding import PartitionSpec as P

BR = 8
MAXOFF = 2
MESH = pl.DeviceIdType.MESH
F32 = jnp.float32
BF16 = jnp.bfloat16


def build_bands(psf_ref, taps, size, bands):
    radius = size // 2
    half = 128
    for image in range(2):
        for part in range(2):
            bands[image, part, :, 0:half, half:] = jnp.zeros((size, half, half), BF16)
            bands[image, part, :, half:, 0:half] = jnp.zeros((size, half, half), BF16)

    def fill(a, carry):
        def place(rows, cols, shift, spots):
            diff = (
                lax.broadcasted_iota(jnp.int32, (rows, cols), 0)
                - lax.broadcasted_iota(jnp.int32, (rows, cols), 1)
                + shift
            )
            value = jnp.zeros((rows, cols), F32)
            for b in range(size):
                value = jnp.where(diff == b - radius, psf_ref[a, b], value)
            for image in range(2):
                full = value if image == 0 else value * value
                high = full.astype(BF16)
                low = (full - high.astype(F32)).astype(BF16)
                for row, col in spots:
                    bands[image, 0, a, row : row + rows, col : col + cols] = high
                    bands[image, 1, a, row : row + rows, col : col + cols] = low

        place(half, half, 0, ((0, 0), (half, half)))
        place(16, half, -16, ((half - 16, half),))
        place(16, half, half, ((half, 0),))
        return carry

    lax.fori_loop(0, size, fill, 0)


def kernel(
    sky_count,
    psf_ref,
    off_ref,
    sci_hbm,
    inv_hbm,
    out_ref,
    sci_ref,
    inv_ref,
    raw,
    high,
    low,
    bands,
    images,
    spill,
    part_send,
    part_own,
    part_recv,
    x_recv,
    load_sems,
    raw_send_sem,
    raw_recv_sem,
    core_send_sem,
    core_recv_sem,
    x_send_sem,
    x_recv_sem,
    spill_send_sem,
    spill_recv_sem,
):
    visits, rows, cols = sci_ref.shape
    size = psf_ref.shape[0]
    radius = size // 2
    halo = radius + BR
    blocks = rows // BR
    velocities = off_ref.shape[0]
    sky = lax.axis_index("sky")
    me = lax.axis_index("visit")
    far, near = lax.div(me, 2), lax.rem(me, 2)
    mate = (sky, 2 * far + 1 - near)
    across = (sky, 2 * (1 - far) + near)
    above, below = (sky - 1, me), (sky + 1, me)
    has_above, has_below = sky > 0, sky < sky_count - 1

    load_sci = pltpu.make_async_copy(sci_hbm, sci_ref, load_sems.at[0])
    load_inv = pltpu.make_async_copy(inv_hbm, inv_ref, load_sems.at[1])
    load_sci.start()
    load_inv.start()

    barrier = pltpu.get_barrier_semaphore()
    pl.semaphore_signal(barrier, inc=1, device_id=mate, device_id_type=MESH)
    pl.semaphore_signal(barrier, inc=1, device_id=across, device_id_type=MESH)

    @pl.when(has_above)
    def _():
        pl.semaphore_signal(barrier, inc=1, device_id=above, device_id_type=MESH)

    @pl.when(has_below)
    def _():
        pl.semaphore_signal(barrier, inc=1, device_id=below, device_id_type=MESH)

    def turn(first, count):
        def block(i, carry):
            at = pl.multiple_of(i * BR, BR)
            variance = inv_ref[:, pl.ds(at, BR), :]
            weighted = sci_ref[:, pl.ds(at, BR), :] * variance
            raw[0, pl.ds(halo + at, BR)] = jnp.swapaxes(weighted, 0, 1)
            raw[1, pl.ds(halo + at, BR)] = jnp.swapaxes(variance, 0, 1)
            return carry

        lax.fori_loop(first, first + count, block, 0)

    def remote(src, dst, send_sem, recv_sem, device):
        return pltpu.make_async_remote_copy(
            src_ref=src,
            dst_ref=dst,
            send_sem=send_sem,
            recv_sem=recv_sem,
            device_id=device,
            device_id_type=MESH,
        )

    up = [
        remote(
            raw.at[:, halo : 2 * halo],
            raw.at[:, halo + rows :],
            raw_send_sem.at[0, 0],
            raw_recv_sem.at[0, 0],
            above,
        ),
    ]
    down = [
        remote(
            raw.at[:, rows : rows + halo],
            raw.at[:, 0:halo],
            raw_send_sem.at[1, 0],
            raw_recv_sem.at[1, 0],
            below,
        ),
    ]
    edge_blocks = (halo + BR - 1) // BR

    def depart(chunk):
        @pl.when(has_above)
        def _():
            up[chunk].start()

        @pl.when(has_below)
        def _():
            down[chunk].start()

    load_sci.wait()
    load_inv.wait()
    turn(0, edge_blocks)
    turn(blocks - edge_blocks, edge_blocks)
    pl.semaphore_wait(barrier, 2 + has_above.astype(jnp.int32) + has_below.astype(jnp.int32))

    depart(0)

    @pl.when(jnp.logical_not(has_above))
    def _():
        raw[:, 0:halo] = jnp.zeros((2, halo, visits, cols), F32)

    @pl.when(jnp.logical_not(has_below))
    def _():
        raw[:, halo + rows :] = jnp.zeros((2, halo, visits, cols), F32)

    turn(edge_blocks, blocks - 2 * edge_blocks)
    build_bands(psf_ref, size, size, bands)

    def split(odd, first, last):
        def pairs_of(first, count):
            for image in range(2):
                rows_in = raw[image, pl.ds(2 * first + odd, 2 * count)]
                pairs = rows_in.reshape(count, 2 * visits, cols)
                head = pairs.astype(BF16)
                high[image, odd, pl.ds(first, count)] = head
                low[image, odd, pl.ds(first, count)] = (pairs - head.astype(F32)).astype(BF16)

        step = 4

        def several(i, carry):
            pairs_of(first + step * i, step)
            return carry

        steps = (last - first) // step
        lax.fori_loop(0, steps, several, 0)
        if first + step * steps < last:
            pairs_of(first + step * steps, last - first - step * steps)

    def correlate(starts, count):
        def image_of(image, carry):
            total = jnp.zeros((len(starts) * count * visits, cols), F32)
            for a in range(size):

                def rows_of(terms):
                    pieces = [
                        terms[image, a % 2, (start + a) // 2 : (start + a) // 2 + count // 2].reshape(
                            count * visits, cols
                        )
                        for start in starts
                    ]
                    return pieces[0] if len(pieces) == 1 else jnp.concatenate(pieces, axis=0)

                x_high, x_low = rows_of(high), rows_of(low)
                w_high, w_low = bands[image, 0, a], bands[image, 1, a]
                total = total + jnp.dot(x_high, w_high, preferred_element_type=F32)
                total = total + jnp.dot(x_low, w_high, preferred_element_type=F32)
                total = total + jnp.dot(x_high, w_low, preferred_element_type=F32)
            value = jnp.swapaxes(total.reshape(len(starts) * count, visits, cols), 0, 1)
            value = value.reshape(visits, len(starts) * count // BR, BR, cols)
            many = count // BR
            for i, start in enumerate(starts):
                images[image, :, 1 + start // BR : 1 + start // BR + many] = value[:, i * many : (i + 1) * many]
            return carry

        lax.fori_loop(0, 2, image_of, 0)

    def stack(block, target):
        def velocity(k, carry):
            totals = [None, None]
            for t in range(visits):
                place = block + MAXOFF + off_ref[k, me * visits + t]
                for image in range(2):
                    term = images[image, t, place]
                    totals[image] = term if t == 0 else totals[image] + term
            target[0, k] = totals[0]
            target[1, k] = totals[1]
            return carry

        lax.fori_loop(0, velocities, velocity, 0, unroll=4)

    core = [
        remote(
            part_send.at[stage],
            part_recv.at[stage],
            core_send_sem.at[stage],
            core_recv_sem.at[stage],
            mate,
        )
        for stage in range(4)
    ]
    hop = [
        remote(
            part_own.at[stage],
            x_recv.at[stage % 2],
            x_send_sem.at[stage % 2],
            x_recv_sem.at[stage % 2],
            across,
        )
        for stage in range(4)
    ]
    middle, last = blocks // 2, blocks - 1
    mine = [
        middle - near,
        middle + 1 - 3 * near,
        1 + (last - 2) * near,
        last * near,
    ]
    other = [last - block for block in mine]
    early_goes = far == near

    def give(stage):
        stack(other[stage], part_send.at[stage])
        core[stage].start()

    def keep(stage):
        stack(mine[stage], part_own.at[stage])

    def gather(stage):
        core[stage].wait_recv()

        def add(k, carry):
            for image in range(2):
                part_own[stage, image, k] += part_recv[stage, image, k]
            return carry

        lax.fori_loop(0, velocities, add, 0, unroll=4)

        @pl.when(early_goes if stage < 2 else jnp.logical_not(early_goes))
        def _():
            hop[stage].start()

    def spread(way, slot):
        source = MAXOFF + blocks - 2 - (blocks - 3) * way
        wanted = 2 * MAXOFF * way - MAXOFF

        def velocity(k, carry):
            totals = [None, None]
            for t in range(visits):
                place = jnp.where(off_ref[k, me * visits + t] == wanted, source, 0)
                for image in range(2):
                    term = images[image, t, place]
                    totals[image] = term if t == 0 else totals[image] + term
            spill[slot, 0, k] = totals[0]
            spill[slot, 1, k] = totals[1]
            return carry

        lax.fori_loop(0, velocities, velocity, 0, unroll=4)

    def spill_copy(src, dst, device):
        return remote(spill.at[src], spill.at[dst], spill_send_sem.at[dst - 2], spill_recv_sem.at[dst - 2], device)

    spill_core = spill_copy(0, 2, mate)
    spill_hop = spill_copy(1, 3, across)
    spill_on = spill_copy(1, 4, (sky + 1 - 2 * near, me))
    passes = jnp.logical_and(early_goes, jnp.where(near == 0, has_below, has_above))
    takes = jnp.where(near == 0, has_above, has_below)

    def arrived(chunk):
        @pl.when(has_above)
        def _():
            down[chunk].wait_recv()

        @pl.when(has_below)
        def _():
            up[chunk].wait_recv()

    def outside(block):
        @pl.when(jnp.logical_not(has_above))
        def _():
            images[:, :, block] = jnp.zeros((2, visits, BR, cols), F32)

        @pl.when(jnp.logical_not(has_below))
        def _():
            images[:, :, blocks + 2 * MAXOFF - 1 - block] = jnp.zeros((2, visits, BR, cols), F32)

    depth = rows + 2 * halo
    lead = 2 * BR
    lo, hi = lead // 2, (depth - lead) // 2
    split(0, lo, hi)
    split(1, lo, hi)
    correlate((lead,), rows + 2 * BR - 2 * lead)
    images[:, :, 0] = jnp.zeros((2, visits, BR, cols), F32)
    images[:, :, blocks + 2 * MAXOFF - 1] = jnp.zeros((2, visits, BR, cols), F32)
    spread(1 - near, 0)
    spill_core.start()
    spread(near, 1)
    give(0)
    keep(0)
    spill_core.wait_recv()

    def join(k, carry):
        for image in range(2):
            spill[1, image, k] += spill[2, image, k]
        return carry

    lax.fori_loop(0, velocities, join, 0, unroll=4)

    @pl.when(jnp.logical_not(early_goes))
    def _():
        spill_hop.start()

    gather(0)
    arrived(0)
    split(0, 0, lo)
    split(1, 0, lo)
    split(0, hi, depth // 2)
    split(1, hi, depth // 2 - 1)
    correlate((0, rows), lead)
    outside(1)

    @pl.when(early_goes)
    def _():
        spill_hop.wait_recv()
        spill[1] += spill[3]

    @pl.when(passes)
    def _():
        spill_on.start()

    give(1)
    give(2)
    keep(1)
    gather(1)
    keep(2)
    gather(2)

    give(3)
    keep(3)
    gather(3)

    def finish(stage, place):
        hop[stage].wait_recv()

        def velocity(k, carry):
            top = part_own[stage, 0, k] + x_recv[stage % 2, 0, k]
            bottom = part_own[stage, 1, k] + x_recv[stage % 2, 1, k]
            out_ref[k, place] = top / jnp.sqrt(bottom)
            return carry

        lax.fori_loop(0, velocities, velocity, 0, unroll=4)

    @pl.when(early_goes)
    def _():
        finish(2, 1 - near)

        @pl.when(takes)
        def _():
            spill_on.wait_recv()
            part_own[3] += spill[4]

        finish(3, near)

    @pl.when(jnp.logical_not(early_goes))
    def _():
        finish(0, near)
        finish(1, 1 - near)

    for chunk in range(1):

        @pl.when(has_above)
        def _():
            up[chunk].wait_send()

        @pl.when(has_below)
        def _():
            down[chunk].wait_send()

    for stage in range(4):
        core[stage].wait_send()
    hop[0].wait_send()
    hop[1].wait_send()
    spill_core.wait_send()

    @pl.when(jnp.logical_not(early_goes))
    def _():
        spill_hop.wait_send()

    @pl.when(passes)
    def _():
        spill_on.wait_send()


def solution(mesh):
    sky_count = mesh.shape["sky"]

    def shards(science, inv_variance, psf_kernel, offsets):
        visits, rows, cols = science.shape
        size = psf_kernel.shape[0]
        velocities = offsets.shape[1]
        group = rows // 4
        depth = rows + 2 * (size // 2 + BR)
        hbm = pl.BlockSpec(memory_space=pltpu.HBM)
        vmem = pl.BlockSpec(memory_space=pltpu.VMEM)
        smem = pl.BlockSpec(memory_space=pltpu.SMEM)
        parts = (4, 2, velocities, BR, cols)
        dma = pltpu.SemaphoreType.DMA

        def body(*refs):
            kernel(sky_count, *refs)

        stacked = pl.pallas_call(
            body,
            out_shape=jax.ShapeDtypeStruct((velocities, group // BR, BR, cols), F32),
            in_specs=[smem, smem, hbm, hbm],
            out_specs=vmem,
            scratch_shapes=[
                pltpu.VMEM((visits, rows, cols), F32),
                pltpu.VMEM((visits, rows, cols), F32),
                pltpu.VMEM((2, depth, visits, cols), F32),
                pltpu.VMEM((2, 2, depth // 2, 2 * visits, cols), BF16),
                pltpu.VMEM((2, 2, depth // 2, 2 * visits, cols), BF16),
                pltpu.VMEM((2, 2, size, cols, cols), BF16),
                pltpu.VMEM((2, visits, rows // BR + 2 * MAXOFF, BR, cols), F32),
                pltpu.VMEM((5,) + parts[1:], F32),
                pltpu.VMEM(parts, F32),
                pltpu.VMEM(parts, F32),
                pltpu.VMEM(parts, F32),
                pltpu.VMEM((2,) + parts[1:], F32),
                dma((2,)),
                dma((2, 2)),
                dma((2, 2)),
                dma((4,)),
                dma((4,)),
                dma((2,)),
                dma((2,)),
                dma((3,)),
                dma((3,)),
            ],
            compiler_params=pltpu.CompilerParams(
                collective_id=0, has_side_effects=True, vmem_limit_bytes=63 * 1024 * 1024
            ),
        )(psf_kernel, offsets.T, science, inv_variance)
        return stacked.reshape(velocities, group, cols)

    return jax.shard_map(
        shards,
        mesh=mesh,
        in_specs=(P("visit", "sky", None), P("visit", "sky", None), P(), P()),
        out_specs=P(None, ("sky", "visit"), None),
        check_vma=False,
    )
```
